32 devices in a mesh: group: 2 (over x), expert: 16 (over z, y, core).
Axes of the slice: x: 2, y: 2, z: 4, core: 2. Of those that a mesh axis runs over, the one named last changes fastest.
Arguments:
- source_tokens: bfloat16 [8192, 2048], P(('group', 'expert')), parts along dimension 0, may hold values from -36 to 36
- routes: int32 [8192, 2], P(('group', 'expert')), parts along dimension 0, may hold values from 0 to 3, all different within a row; in each aligned block of 256 rows (0 to 255, 256 to 511, ...) at most 192 rows name the same one
- source_lengths: int32 [32, 4], P(('group', 'expert')), parts along dimension 0, may hold values from 1 to 192, 256 in all within a row
- router_weight: bfloat16 [2048, 4], replicated, may hold values from -0.125 to 0.125
- expert_in: bfloat16 [16, 2048, 1024], P('expert'), may hold values from -0.125 to 0.125
- expert_out: bfloat16 [16, 1024, 2048], P('expert'), may hold values from -0.09375 to 0.09375
- memory_weight: bfloat16 [2048, 2048], replicated, may hold values from -0.125 to 0.125
- decode_inputs: bfloat16 [2, 192, 2048], P(None, ('group', 'expert')), parts along dimension 1, may hold values from -36 to 36
- self_cache: bfloat16 [192, 64, 2048], P(('group', 'expert')), parts along dimension 0, may hold values from -6 to 6
- context_lengths: int32 [192], P(('group', 'expert')), parts along dimension 0, may hold values from 1 to 64, as said below
- old_memory: bfloat16 [64, 192, 2048], P(('group', 'expert')), parts along dimension 0, may hold values from -6 to 6
- old_lengths: int32 [64], P(('group', 'expert')), parts along dimension 0, may hold values from 1 to 192, as said below
- slot_of: int32 [192], P('group'), parts along dimension 0, may hold values from 0 to 95, each once
- qkv_weight: bfloat16 [2048, 3072], P('expert'), may hold values from -0.125 to 0.125
- self_out_weight: bfloat16 [1024, 2048], P('expert'), may hold values from -0.1875 to 0.1875
- cross_query_weight: bfloat16 [2048, 1024], P('expert'), may hold values from -0.125 to 0.125
- cross_out_weight: bfloat16 [1024, 2048], P('expert'), may hold values from -0.1875 to 0.1875
Outputs:
- encoded: bfloat16 [8192, 2048], P(('group', 'expert')), parts along dimension 0
- decoded: bfloat16 [2, 192, 2048], P(None, ('group', 'expert')), parts along dimension 1
The draws below stay inside these ranges and needn't reach their ends.
There are 2 independent parts, one for each index of `group`. The reference program is written for one: setup_inputs(seed, part) draws one part's arguments, and reference() takes and returns one part's arrays. A program takes and returns all parts, laid end to end along the dimension named above; an argument that names none is the same for every part. Nothing has to cross between parts.
Inputs may be any that keep to these rules, and one draw needn't show every extreme that they name: `routes`: within the rows of any device no expert is named more than 192 times, and on some device some expert reaches 192; a row names two different experts. `source_lengths`: each row sums to 256 and its largest entry is exactly 192. `context_lengths`: some slot holds exactly 64. `old_lengths`: some running request reaches 192. `slot_of`: each slot once.
All inputs are finite; a program needn't handle non-finite values.
Results may differ from the reference program's by a relative error of at most 0.0039.
Values may be sent and summed in bfloat16 or wider, within the bound.
No kernel may reach another device: no remote copies, remote signals or barrier semaphores. Data moves between devices by JAX's collectives and lax.ppermute only.
A program may use at most 128 MiB of HBM per device.

```python
import math
import jax
import jax.numpy as jnp
import numpy as np
from jax import lax

D = 2048
HEADS = 8
HD = 128
FF = 4096
EXP_SPLIT = 4
SRC_DEV = 4
OLD_DEV = 2
TOK_DEV = 256
CTX = 64
EXPERTS = 4
FF_DEV = 1024
KV = 1024
CAP = 192
SRC_MAX = 192
HELD = 6
SLOTS = 96
TOKENS = 4096
OLD_SRCS = 32
N_EXPERT = 16


def draw_source_tokens(key, part):
    key = jax.random.fold_in(key, 11)
    subkeys = jax.random.split(key, 5)
    row_scale = jnp.exp(jax.random.uniform(subkeys[0], (TOKENS, 1), jnp.float32, -1.2, 1.1))
    columns = jnp.exp(jax.random.uniform(subkeys[1], (1, D), jnp.float32, -1.2, 1.1))
    noise_part = jnp.clip(jax.random.normal(subkeys[4], (TOKENS, D), jnp.float32), -4.0, 4.0)
    return (noise_part * row_scale * columns).astype(jnp.bfloat16)


def draw_decode_inputs(key, part):
    key = jax.random.fold_in(key, 17)
    subkeys = jax.random.split(key, 5)
    row_scale = jnp.exp(jax.random.uniform(subkeys[0], (2, SLOTS, 1), jnp.float32, -1.2, 1.1))
    columns = jnp.exp(jax.random.uniform(subkeys[1], (1, 1, D), jnp.float32, -1.2, 1.1))
    noise_part = jnp.clip(jax.random.normal(subkeys[4], (2, SLOTS, D), jnp.float32), -4.0, 4.0)
    return (noise_part * row_scale * columns).astype(jnp.bfloat16)


def draw_context_lengths(key, part):
    key = jax.random.fold_in(key, 23)
    length_key, place_key = jax.random.split(key)
    drawn_lengths = jax.random.randint(length_key, (SLOTS,), 1, CTX + 1, dtype=jnp.int32)
    picked_slot = jax.random.randint(place_key, (), 0, SLOTS, dtype=jnp.int32)
    return jnp.where(jnp.arange(SLOTS, dtype=jnp.int32) == picked_slot, CTX, drawn_lengths).astype(jnp.int32)


def draw_old_lengths(key, part):
    key = jax.random.fold_in(key, 29)
    length_key, place_key = jax.random.split(key)
    drawn_lengths = jax.random.randint(length_key, (OLD_SRCS,), 1, SRC_MAX + 1, dtype=jnp.int32)
    picked_slot = jax.random.randint(place_key, (), 0, OLD_SRCS, dtype=jnp.int32)
    return jnp.where(jnp.arange(OLD_SRCS, dtype=jnp.int32) == picked_slot, SRC_MAX, drawn_lengths).astype(jnp.int32)


def block_levels(own_key, extent, pieces, least, high):
    level, own = 1.0, jax.random.fold_in(own_key, 6)
    for axis_at, blocks in pieces:
        heights = jnp.exp(jax.random.uniform(jax.random.fold_in(own, axis_at), (blocks,), jnp.float32, least / len(pieces), high / len(pieces)))
        level = level * jnp.repeat(heights, extent[axis_at] // blocks).reshape([-1 if axis == axis_at else 1 for axis in range(len(extent))])
    return level


def split_up(amount, total, most, lean):
    weights = [(1 << 20) // math.isqrt(standing ** lean) + 1 for standing in range(2, amount + 1)]
    rest, counts = total - most - (amount - 1), [1] * (amount - 1)
    while rest > 0:
        candidates = [i for i in range(amount - 1) if counts[i] < most]
        whole, left = sum([weights[i] for i in candidates]), rest
        for i in candidates:
            more = min(most - counts[i], max(1, left * weights[i] // whole), rest)
            counts[i] = counts[i] + more
            rest = rest - more
    return np.array([most] + counts)


def ragged(own_key, number_of, total, reach, lean):
    if number_of == 2:
        one = jax.random.randint(own_key, (), max(1, total - reach), min(reach, total - 1) + 1)
        return jnp.stack([one, total - one])
    lengths = jnp.asarray(split_up(number_of, total, reach, lean), jnp.int32)
    couples = (number_of - 1) // 2
    source_of, receiver = lengths[1:1 + 2 * couples:2], lengths[2:2 + 2 * couples:2]
    margin = jnp.minimum(source_of - 1, reach - receiver)
    shifted = jax.random.randint(jax.random.fold_in(own_key, 1), (couples,), 0, 1 << 20) % (margin + 1)
    lengths = lengths.at[1:1 + 2 * couples:2].set(source_of - shifted).at[2:2 + 2 * couples:2].set(receiver + shifted)
    return lengths[jax.random.permutation(jax.random.fold_in(own_key, 2), number_of)]


def shared_out(key, own, number, rows, number_of, top, reach, lean):
    sequence = jax.random.permutation(key, number_of)
    heavy_load, usual = shares(number_of, rows * top, reach, lean, True), shares(number_of, rows * top, reach, lean, False)
    places = jnp.arange(number_of)

    def named(lengths, offset_by):
        used = int((lengths > 0).sum())
        fixed = max(1, used // 4)
        moved = fixed + (places - fixed + offset_by * (used - fixed)) % max(1, number_of - fixed)
        return jnp.zeros((number_of,), jnp.int32).at[sequence[jnp.where(places < fixed, places, moved)]].set(jnp.asarray(lengths, jnp.int32))

    lengths = jnp.where(number % 4 == 0, named(heavy_load, number // 4), named(usual, number - number // 4 - 1))
    mixed = jax.random.permutation(jax.random.fold_in(own, 3), number_of)
    donor, sink = mixed[0:number_of // 2 * 2:2], mixed[1:number_of // 2 * 2:2]
    margin = jnp.minimum(lengths[donor] - 1, reach - lengths[sink]) // 2
    margin = jnp.where((donor == sequence[0]) | (sink == sequence[0]) | (lengths[sink] == 0), 0, jnp.maximum(margin, 0))
    moved = jax.random.randint(jax.random.fold_in(own, 4), (number_of // 2,), 0, 1 << 20) % (margin + 1)
    lengths = lengths.at[donor].add(-moved).at[sink].add(moved)
    items = jnp.searchsorted(jnp.cumsum(lengths), jnp.arange(rows * top), side="right").astype(jnp.int32)
    listing = items.reshape(top, rows).T
    listing = listing[jax.random.permutation(jax.random.fold_in(own, 1), rows)]
    offset_by = jax.random.randint(jax.random.fold_in(own, 2), (rows, 1), 0, top)
    return jnp.take_along_axis(listing, (jnp.arange(top)[None, :] + offset_by) % top, axis=1)


def shares(number_of, total, bound, slope, full):
    loads = [(1 << 20) // math.isqrt(grade ** slope) + 1 for grade in range(1, number_of + 1)]
    largest = bound if full else min(bound, max(-(-total // number_of), total * loads[0] // sum(loads)))
    least = 1 if total - largest >= number_of - 1 else 0
    given, rest = [largest] + [least] * (number_of - 1), total - largest - least * (number_of - 1)
    while rest > 0:
        free = [i for i in range(1, number_of) if given[i] < largest] or [i for i in range(1, number_of) if given[i] < bound]
        pool, remaining = sum([loads[i] for i in free]), rest
        for i in free:
            more = min(bound - given[i], max(1, remaining * loads[i] // pool), rest)
            given[i] = given[i] + more
            rest = rest - more
    return np.array(given)


def gaussian(key, shape, scale, bound, pieces=(), kind=jnp.bfloat16):
    level = block_levels(key, shape, pieces, -0.22, 0.18) if pieces else 1.0
    values = jax.random.normal(key, shape, jnp.float32) * scale * level
    return jnp.minimum(jnp.maximum(values, -bound), bound).astype(kind)


def setup_inputs(seed: int = 0, part: int = 0) -> dict:
    key_list = jax.random.split(jax.random.key(seed), 18)
    part_keys = jax.random.split(jax.random.fold_in(key_list[17], part), 18)
    source_tokens = draw_source_tokens(jax.random.fold_in(jax.random.fold_in(key_list[17], part), 71), part)
    routes_keys = jax.random.split(jax.random.fold_in(part_keys[1], 1), TOKENS // TOK_DEV)
    routes_turns = jax.random.permutation(jax.random.fold_in(part_keys[1], 3), TOKENS // TOK_DEV)
    routes = jax.vmap(lambda own, number: shared_out(jax.random.fold_in(part_keys[1], 2), own, number, TOK_DEV, EXPERTS, 2, CAP, 2))(routes_keys, routes_turns).reshape((TOKENS, 2))
    source_lengths = jax.vmap(lambda own: ragged(own, SRC_DEV, TOK_DEV, SRC_MAX, 2))(jax.random.split(part_keys[2], N_EXPERT)).reshape((N_EXPERT, SRC_DEV)).astype(jnp.int32)
    router_weight = gaussian(key_list[3], (D, EXPERTS), D ** -0.5, 0.125)
    expert_in = gaussian(key_list[4], (N_EXPERT, D, FF_DEV), D ** -0.5, 0.125, ((0, 16),))
    expert_out = gaussian(key_list[5], (N_EXPERT, FF_DEV, D), FF ** -0.5, 0.09375, ((0, 16),))
    memory_weight = gaussian(key_list[6], (D, 2 * KV), D ** -0.5, 0.125)
    decode_inputs = draw_decode_inputs(jax.random.fold_in(jax.random.fold_in(key_list[17], part), 71), part)
    self_cache = gaussian(part_keys[8], (SLOTS, CTX, 2 * KV), 1.0, 6.0, ((0, 16),))
    context_lengths = draw_context_lengths(jax.random.fold_in(jax.random.fold_in(key_list[17], part), 71), part)
    old_memory = gaussian(part_keys[10], (OLD_SRCS, SRC_MAX, 2 * KV), 1.0, 6.0, ((0, 16),))
    old_lengths = draw_old_lengths(jax.random.fold_in(jax.random.fold_in(key_list[17], part), 71), part)
    slot_of = jax.random.permutation(part_keys[12], SLOTS).astype(jnp.int32)
    qkv_weight = gaussian(key_list[13], (D, 3 * KV), D ** -0.5, 0.125, ((0, 16),))
    self_out_weight = gaussian(key_list[14], (KV, D), KV ** -0.5, 0.1875, ((0, 16),))
    cross_query_weight = gaussian(key_list[15], (D, KV), D ** -0.5, 0.125, ((0, 16),))
    cross_out_weight = gaussian(key_list[16], (KV, D), KV ** -0.5, 0.1875, ((0, 16),))
    return dict(source_tokens=source_tokens, routes=routes, source_lengths=source_lengths, router_weight=router_weight, expert_in=expert_in, expert_out=expert_out, memory_weight=memory_weight, decode_inputs=decode_inputs, self_cache=self_cache, context_lengths=context_lengths, old_memory=old_memory, old_lengths=old_lengths, slot_of=slot_of, qkv_weight=qkv_weight, self_out_weight=self_out_weight, cross_query_weight=cross_query_weight, cross_out_weight=cross_out_weight)


def normalized(values):
    values = values.astype(jnp.float32)
    average = lax.optimization_barrier(jnp.mean(values, axis=-1, keepdims=True))
    centred = values - average
    variance = lax.optimization_barrier(jnp.mean(centred * centred, axis=-1, keepdims=True))
    return centred * lax.rsqrt(variance + 1e-05)

def rounded_sum(running, partial_value):
    return running + lax.optimization_barrier(partial_value.astype(jnp.bfloat16)).astype(jnp.float32)

def attend_shared(queries, all_keys, all_values, key_mask):
    scores = jnp.einsum('phd,jhd->phj', queries.astype(jnp.float32), all_keys.astype(jnp.float32)) * HD ** (-0.5)
    raised = jnp.exp(scores) * key_mask[:, None, :]
    weights_bf = (raised / lax.optimization_barrier(jnp.sum(raised, axis=-1, keepdims=True))).astype(jnp.bfloat16)
    result = jnp.einsum('phj,jhd->phd', weights_bf.astype(jnp.float32), all_values.astype(jnp.float32))
    return result.astype(jnp.bfloat16)

def encoder_layer(source_tokens, routes, router_weight, expert_in, expert_out):
    hidden_rows = normalized(source_tokens).astype(jnp.bfloat16)
    logits = jnp.dot(hidden_rows, router_weight, preferred_element_type=jnp.float32)
    chosen = jnp.take_along_axis(logits, routes, axis=1)
    leading = jax.nn.sigmoid(chosen[:, 0] - chosen[:, 1])
    gate_values = jnp.stack([leading, 1.0 - leading], axis=1).reshape(-1)
    flat_routes = routes.reshape(-1)
    token_of = jnp.arange(TOKENS * 2, dtype=jnp.int32) // 2
    row_bound = N_EXPERT * CAP

    def per_expert(running, expert_id):
        member = flat_routes == expert_id
        picked = jnp.nonzero(member, size=row_bound, fill_value=0)[0].astype(jnp.int32)
        valid_rows = jnp.arange(row_bound, dtype=jnp.int32) < jnp.sum(member.astype(jnp.int32))
        row_weights = jnp.where(valid_rows, gate_values[picked], 0.0)
        token_rows = token_of[picked]
        inputs = hidden_rows[token_rows]
        summed = jnp.zeros((row_bound, D), jnp.float32)
        for piece_index in range(EXP_SPLIT):
            weight_row = expert_id * EXP_SPLIT + piece_index
            activated = jnp.maximum(jnp.dot(inputs, expert_in[weight_row], preferred_element_type=jnp.float32), 0.0).astype(jnp.bfloat16)
            summed = rounded_sum(summed, jnp.dot(activated, expert_out[weight_row], preferred_element_type=jnp.float32))
        return (running.at[token_rows].add(row_weights[:, None] * summed), None)
    expert_sum, unused = lax.scan(per_expert, jnp.zeros((TOKENS, D), jnp.float32), jnp.arange(EXPERTS, dtype=jnp.int32))
    return source_tokens.astype(jnp.float32) + expert_sum

def reference(source_tokens, routes, source_lengths, router_weight, expert_in, expert_out, memory_weight, decode_inputs, self_cache, context_lengths, old_memory, old_lengths, slot_of, qkv_weight, self_out_weight, cross_query_weight, cross_out_weight):
    encoder_sum = encoder_layer(source_tokens, routes, router_weight, expert_in, expert_out)
    encoded = encoder_sum.astype(jnp.bfloat16)
    memory = normalized(encoder_sum).astype(jnp.bfloat16)
    memory_kv = jnp.dot(memory, memory_weight, preferred_element_type=jnp.float32).astype(jnp.bfloat16)
    new_keys = memory_kv[:, :KV].reshape(N_EXPERT, TOK_DEV, HEADS, HD)
    new_values = memory_kv[:, KV:].reshape(N_EXPERT, TOK_DEV, HEADS, HD)
    bounds = jnp.cumsum(source_lengths, axis=1)
    segment = lax.optimization_barrier(jnp.sum((jnp.arange(TOK_DEV, dtype=jnp.int32)[None, :, None] >= bounds[:, None, :]).astype(jnp.int32), axis=-1))
    new_mask = (segment[:, None, :] == jnp.arange(SRC_DEV, dtype=jnp.int32)[None, :, None]).astype(jnp.float32)
    old_keys = old_memory[:, :, :KV].reshape(OLD_SRCS, SRC_MAX, HEADS, HD)
    old_values = old_memory[:, :, KV:].reshape(OLD_SRCS, SRC_MAX, HEADS, HD)
    old_mask = (jnp.arange(SRC_MAX, dtype=jnp.int32)[None, :] < old_lengths[:, None]).astype(jnp.float32)[:, None, :]
    new_slots = slot_of.reshape(N_EXPERT, HELD)[:, :SRC_DEV].reshape(-1)
    fresh_slot = jnp.zeros((SLOTS,), jnp.bool_).at[new_slots].set(True)
    effective = jnp.where(fresh_slot, 0, context_lengths)
    cache_mask = (jnp.arange(CTX, dtype=jnp.int32)[None, :] < effective[:, None]).astype(jnp.float32)
    cache_keys = self_cache[:, :, :KV].reshape(SLOTS, CTX, HEADS, HD)
    cache_values = self_cache[:, :, KV:].reshape(SLOTS, CTX, HEADS, HD)
    normed_inputs = normalized(decode_inputs).astype(jnp.bfloat16)
    projected_qkv = jnp.dot(normed_inputs.reshape(2 * SLOTS, D), qkv_weight, preferred_element_type=jnp.float32)
    projected_qkv = projected_qkv.astype(jnp.bfloat16).reshape(2, SLOTS, 3, HEADS, HD)
    outputs = []
    for step_index in range(2):
        queries = projected_qkv[step_index, :, 0]
        all_keys = jnp.concatenate([cache_keys, jnp.transpose(projected_qkv[:step_index + 1, :, 1], (1, 0, 2, 3))], axis=1)
        all_values = jnp.concatenate([cache_values, jnp.transpose(projected_qkv[:step_index + 1, :, 2], (1, 0, 2, 3))], axis=1)
        key_mask = jnp.concatenate([cache_mask, jnp.ones((SLOTS, step_index + 1), jnp.float32)], axis=1)
        attended = jax.vmap(attend_shared)(queries[:, None], all_keys, all_values, key_mask[:, None, :]).reshape(SLOTS, KV)
        after_self = decode_inputs[step_index].astype(jnp.float32) + jnp.dot(attended, self_out_weight, preferred_element_type=jnp.float32)
        normed_self = normalized(after_self).astype(jnp.bfloat16)
        cross_queries = jnp.dot(normed_self, cross_query_weight, preferred_element_type=jnp.float32).astype(jnp.bfloat16)
        held_queries = cross_queries[slot_of].reshape(N_EXPERT, HELD, HEADS, HD)
        new_out = jax.vmap(attend_shared)(held_queries[:, :SRC_DEV], new_keys, new_values, new_mask)
        old_queries = held_queries[:, SRC_DEV:].reshape(OLD_SRCS, 1, HEADS, HD)
        old_out = jax.vmap(attend_shared)(old_queries, old_keys, old_values, old_mask).reshape(N_EXPERT, OLD_DEV, HEADS, HD)
        held_out = jnp.concatenate([new_out, old_out], axis=1).reshape(SLOTS, KV)
        slot_out = jnp.zeros((SLOTS, KV), jnp.bfloat16).at[slot_of].set(held_out)
        cross_sum = jnp.dot(slot_out, cross_out_weight, preferred_element_type=jnp.float32)
        outputs.append((after_self + cross_sum).astype(jnp.bfloat16))
    return (encoded, jnp.stack(outputs))
```

```python
import jax
import jax.numpy as jnp
from jax import lax
from jax.sharding import PartitionSpec as P

HEADS = 8
HD = 128
EXP_SPLIT = 4
SRC_DEV = 4
OLD_DEV = 2
TOK_DEV = 256
CTX = 64
KV = 1024
SRC_MAX = 192
HELD = 6
STEPS = 2
BF = jnp.bfloat16
F32 = jnp.float32


def normalized(values):
    values = values.astype(jnp.float32)
    average = jnp.mean(values, axis=-1, keepdims=True)
    centred = values - average
    variance = jnp.mean(centred * centred, axis=-1, keepdims=True)
    return centred * lax.rsqrt(variance + 1e-05)


def attend_shared(queries, all_keys, all_values, key_mask):
    scores = jnp.einsum("phd,jhd->phj", queries, all_keys, preferred_element_type=F32) * HD ** (-0.5)
    raised = jnp.exp(scores) * key_mask[:, None, :]
    weights_bf = (raised / jnp.sum(raised, axis=-1, keepdims=True)).astype(BF)
    result = jnp.einsum("phj,jhd->phd", weights_bf, all_values, preferred_element_type=F32)
    return result.astype(BF)


def swap(values, devices, bit):
    return lax.ppermute(values, "expert", [(i, i ^ bit) for i in range(devices)])


def turn(values, devices, distance):
    step = EXP_SPLIT * distance
    return lax.ppermute(values, "expert", [(i, (i + step) % devices) for i in range(devices)])


def turn_order(planes):
    order = []
    for distance in range(1, planes // 2 + 1):
        order.append(distance)
        if planes - distance != distance:
            order.append(planes - distance)
    return order


def summed_rows(partial, devices, own_index):
    planes = devices // EXP_SPLIT
    rows = partial.shape[0] // devices
    blocks = partial.reshape(planes, 2, 2, rows, partial.shape[1])
    core = own_index % 2
    side = (own_index // 2) % 2
    plane = own_index // EXP_SPLIT
    kept = jnp.where(core == 0, blocks[:, :, 0], blocks[:, :, 1])
    sent = jnp.where(core == 0, blocks[:, :, 1], blocks[:, :, 0]).astype(BF)
    kept = kept + swap(sent, devices, 1).astype(F32)
    sent = jnp.where(side == 0, kept[:, 1], kept[:, 0]).astype(BF)
    kept = jnp.where(side == 0, kept[:, 0], kept[:, 1]) + swap(sent, devices, 2).astype(F32)
    total = lax.dynamic_index_in_dim(kept, plane, 0, keepdims=False)
    low = kept.astype(BF)
    for distance in turn_order(planes):
        block = lax.dynamic_index_in_dim(low, (plane + distance) % planes, 0, keepdims=False)
        total = total + turn(block, devices, distance).astype(F32)
    return total


def project(local_rows, weight, order, devices, own_index):
    spread = lax.all_to_all(local_rows, "expert", split_axis=1, concat_axis=0, tiled=True)
    if order is not None:
        spread = jnp.dot(order, spread, preferred_element_type=F32).astype(BF)
    return summed_rows(jnp.dot(spread, weight, preferred_element_type=F32), devices, own_index)


def body(
    source_tokens,
    routes,
    source_lengths,
    router_weight,
    expert_in,
    expert_out,
    memory_weight,
    decode_inputs,
    self_cache,
    context_lengths,
    old_memory,
    old_lengths,
    slot_of,
    qkv_weight,
    self_out_weight,
    cross_query_weight,
    cross_out_weight,
):
    devices = lax.axis_size("expert")
    own_index = lax.axis_index("expert")
    token_count = source_tokens.shape[0]
    expert_count = router_weight.shape[1]
    planes = devices // EXP_SPLIT
    plane = own_index // EXP_SPLIT
    capacity = 3 * token_count // expert_count
    slot_count = decode_inputs.shape[1]

    hidden_rows = normalized(source_tokens).astype(BF)
    logits = jnp.dot(hidden_rows, router_weight, preferred_element_type=F32)
    one_hot = routes[:, :, None] == jnp.arange(expert_count, dtype=jnp.int32)[None, None, :]
    chosen = jnp.sum(jnp.where(one_hot, logits[:, None, :], 0.0), axis=-1)
    leading = jax.nn.sigmoid(chosen[:, 0] - chosen[:, 1])
    member = jnp.any(one_hot, axis=1)
    earlier = (
        jnp.arange(token_count, dtype=jnp.int32)[:, None] > jnp.arange(token_count, dtype=jnp.int32)[None, :]
    ).astype(BF)
    rank = jnp.dot(earlier, member.astype(BF), preferred_element_type=F32).astype(jnp.int32)
    w_in = expert_in[0]
    w_out = expert_out[0]

    def choice(distance):
        target = (plane + distance) % planes
        is_target = jnp.arange(expert_count, dtype=jnp.int32) == target
        there = jnp.any(member & is_target[None, :], axis=1)
        place = jnp.sum(jnp.where(is_target[None, :], rank, 0), axis=1)
        place = jnp.where(there, place, -1)
        gate = jnp.where(routes[:, 0] == target, leading, 0.0) + jnp.where(
            routes[:, 1] == target, 1.0 - leading, 0.0
        )
        return place, gate

    distances = turn_order(planes) + [0]
    spots = jnp.arange(capacity, dtype=jnp.int32)
    choices = {d: choice(d) for d in distances}

    def picked(distance):
        place, _ = choices[distance]
        pick = (place[None, :] == spots[:, None]).astype(BF)
        return jnp.dot(pick, hidden_rows, preferred_element_type=F32).astype(BF)

    back = {}
    for distance in [0] + turn_order(planes):
        block = picked(distance)
        if distance:
            block = turn(block, devices, distance)
        other_side = swap(block, devices, 2)
        other_core = swap(block, devices, 1)
        diagonal = swap(other_side, devices, 1)
        rows = jnp.concatenate([block, other_side, other_core, diagonal], axis=0)
        active = jnp.maximum(jnp.dot(rows, w_in, preferred_element_type=F32), 0.0).astype(BF)
        partial = jnp.dot(active, w_out, preferred_element_type=F32)
        half = partial[: 2 * capacity] + swap(partial[2 * capacity :].astype(BF), devices, 1).astype(F32)
        full = half[:capacity] + swap(half[capacity:].astype(BF), devices, 2).astype(F32)
        full = full.astype(BF)
        back[distance] = turn(full, devices, planes - distance) if distance else full

    global_slots = own_index * slot_count + jnp.arange(slot_count, dtype=jnp.int32)
    new_slots = slot_of.reshape(devices, HELD)[:, :SRC_DEV].reshape(-1)
    fresh_slot = jnp.any(global_slots[:, None] == new_slots[None, :], axis=-1)
    effective = jnp.where(fresh_slot, 0, context_lengths)
    cache_mask = (jnp.arange(CTX, dtype=jnp.int32)[None, :] < effective[:, None]).astype(F32)
    cache_keys = self_cache[:, :, :KV].reshape(slot_count, CTX, HEADS, HD)
    cache_values = self_cache[:, :, KV:].reshape(slot_count, CTX, HEADS, HD)
    count = slot_of.shape[0]
    to_request = (slot_of[:, None] == jnp.arange(count, dtype=jnp.int32)[None, :]).astype(BF)

    def spread_order(matrix):
        by_device = matrix.reshape(devices, HELD, devices, HELD)
        full = by_device[:, None, :, :, None, :] * jnp.eye(STEPS, dtype=BF)[None, :, None, None, :, None]
        return full.reshape(STEPS * count, STEPS * count)

    order_request = spread_order(to_request)
    order_slot = spread_order(to_request.T)

    normed_inputs = normalized(decode_inputs).astype(BF).reshape(STEPS * slot_count, -1)
    current = project(normed_inputs, qkv_weight, None, devices, own_index).astype(BF)
    current = current.reshape(STEPS, slot_count, 3, HEADS, HD).transpose(1, 0, 2, 3, 4)
    all_keys = jnp.concatenate([cache_keys, current[:, :, 1]], axis=1)
    all_values = jnp.concatenate([cache_values, current[:, :, 2]], axis=1)
    steps = jnp.arange(STEPS, dtype=jnp.int32)
    causal = (steps[:, None] >= steps[None, :]).astype(F32)
    key_mask = jnp.concatenate(
        [
            jnp.broadcast_to(cache_mask[:, None, :], (slot_count, STEPS, CTX)),
            jnp.broadcast_to(causal[None], (slot_count, STEPS, STEPS)),
        ],
        axis=2,
    )
    attended = jax.vmap(attend_shared)(current[:, :, 0], all_keys, all_values, key_mask)
    attended = attended.transpose(1, 0, 2, 3).reshape(STEPS * slot_count, KV)
    after_self = decode_inputs.astype(F32).reshape(STEPS * slot_count, -1) + project(
        attended, self_out_weight, None, devices, own_index
    )
    normed_self = normalized(after_self).astype(BF)
    cross_rows = project(normed_self, cross_query_weight, order_request, devices, own_index).astype(BF)
    cross_rows = cross_rows.reshape(STEPS, HELD, HEADS, HD)
    old_keys = old_memory[:, :, :KV].reshape(OLD_DEV, SRC_MAX, HEADS, HD)
    old_values = old_memory[:, :, KV:].reshape(OLD_DEV, SRC_MAX, HEADS, HD)
    old_mask = (jnp.arange(SRC_MAX, dtype=jnp.int32)[None, :] < old_lengths[:, None]).astype(F32)
    old_out = jax.vmap(attend_shared)(
        cross_rows[:, SRC_DEV:].transpose(1, 0, 2, 3),
        old_keys,
        old_values,
        jnp.broadcast_to(old_mask[:, None, :], (OLD_DEV, STEPS, SRC_MAX)),
    ).transpose(1, 0, 2, 3)

    encoder_sum = source_tokens.astype(F32)
    for distance in distances:
        place, gate = choices[distance]
        pick = (place[:, None] == spots[None, :]).astype(BF)
        encoder_sum = encoder_sum + gate[:, None] * jnp.dot(pick, back[distance], preferred_element_type=F32)
    encoded = encoder_sum.astype(BF)
    memory = normalized(encoder_sum).astype(BF)
    memory_kv = jnp.dot(memory, memory_weight, preferred_element_type=F32).astype(BF)
    new_keys = memory_kv[:, :KV].reshape(TOK_DEV, HEADS, HD)
    new_values = memory_kv[:, KV:].reshape(TOK_DEV, HEADS, HD)
    bounds = jnp.cumsum(source_lengths[0])
    segment = jnp.sum(
        (jnp.arange(TOK_DEV, dtype=jnp.int32)[:, None] >= bounds[None, :]).astype(jnp.int32),
        axis=-1,
    )
    new_mask = (segment[None, :] == jnp.arange(SRC_DEV, dtype=jnp.int32)[:, None]).astype(F32)
    new_out = attend_shared(
        cross_rows[:, :SRC_DEV].reshape(STEPS * SRC_DEV, HEADS, HD),
        new_keys,
        new_values,
        jnp.tile(new_mask, (STEPS, 1)),
    ).reshape(STEPS, SRC_DEV, HEADS, HD)
    held_out = jnp.concatenate([new_out, old_out], axis=1).reshape(STEPS * HELD, KV)
    cross_sum = project(held_out, cross_out_weight, order_slot, devices, own_index)
    decoded = (after_self + cross_sum).astype(BF).reshape(STEPS, slot_count, -1)
    return (encoded, decoded)


def solution(mesh):
    return jax.shard_map(
        body,
        mesh=mesh,
        in_specs=(
            P(("group", "expert"), None),
            P(("group", "expert"), None),
            P(("group", "expert"), None),
            P(),
            P("expert", None, None),
            P("expert", None, None),
            P(),
            P(None, ("group", "expert"), None),
            P(("group", "expert"), None, None),
            P(("group", "expert")),
            P(("group", "expert"), None, None),
            P(("group", "expert")),
            P("group"),
            P("expert", None),
            P("expert", None),
            P("expert", None),
            P("expert", None),
        ),
        out_specs=(P(("group", "expert"), None), P(None, ("group", "expert"), None)),
        check_vma=False,
    )
```

```python
import jax
import jax.numpy as jnp
from jax import lax
from jax.sharding import PartitionSpec as P

HEADS = 8
HD = 128
EXP_SPLIT = 4
SRC_DEV = 4
OLD_DEV = 2
TOK_DEV = 256
CTX = 64
KV = 1024
SRC_MAX = 192
HELD = 6
STEPS = 2
BF = jnp.bfloat16
F32 = jnp.float32


def normalized(values):
    values = values.astype(jnp.float32)
    average = jnp.mean(values, axis=-1, keepdims=True)
    centred = values - average
    variance = jnp.mean(centred * centred, axis=-1, keepdims=True)
    return centred * lax.rsqrt(variance + 1e-05)


def attend_shared(queries, all_keys, all_values, key_mask):
    scores = jnp.einsum("phd,jhd->phj", queries, all_keys, preferred_element_type=F32) * HD ** (-0.5)
    raised = jnp.exp(scores) * key_mask[:, None, :]
    weights_bf = (raised / jnp.sum(raised, axis=-1, keepdims=True)).astype(BF)
    result = jnp.einsum("phj,jhd->phd", weights_bf, all_values, preferred_element_type=F32)
    return result.astype(BF)


def swap(values, devices, bit):
    return lax.ppermute(values, "expert", [(i, i ^ bit) for i in range(devices)])


def turn(values, devices, distance):
    step = EXP_SPLIT * distance
    return lax.ppermute(values, "expert", [(i, (i + step) % devices) for i in range(devices)])


def turn_order(planes):
    order = []
    for distance in range(1, planes // 2 + 1):
        order.append(distance)
        if planes - distance != distance:
            order.append(planes - distance)
    return order


def blocks_of(partial, devices):
    rows = partial.shape[0] // devices
    return partial.reshape(devices // EXP_SPLIT, 2, 2, rows, partial.shape[1])


def sum_in_plane(partial, devices, own_index):
    blocks = blocks_of(partial, devices)
    core = own_index % 2
    side = (own_index // 2) % 2
    kept = jnp.where(core == 0, blocks[:, :, 0], blocks[:, :, 1])
    sent = jnp.where(core == 0, blocks[:, :, 1], blocks[:, :, 0]).astype(BF)
    kept = kept + swap(sent, devices, 1).astype(F32)
    sent = jnp.where(side == 0, kept[:, 1], kept[:, 0]).astype(BF)
    return jnp.where(side == 0, kept[:, 0], kept[:, 1]) + swap(sent, devices, 2).astype(F32)


def sum_planes(kept, devices, own_index):
    planes = devices // EXP_SPLIT
    plane = own_index // EXP_SPLIT
    total = lax.dynamic_index_in_dim(kept, plane, 0, keepdims=False)
    low = kept.astype(BF)
    for distance in turn_order(planes):
        block = lax.dynamic_index_in_dim(low, (plane + distance) % planes, 0, keepdims=False)
        total = total + turn(block, devices, distance).astype(F32)
    return total


def spread_features(local_rows):
    return lax.all_to_all(local_rows, "expert", split_axis=1, concat_axis=0, tiled=True)


def reorder(order, spread):
    return jnp.dot(order, spread, preferred_element_type=F32).astype(BF)


def matmul(left, right):
    return jnp.dot(left, right, preferred_element_type=F32)


def body(
    source_tokens,
    routes,
    source_lengths,
    router_weight,
    expert_in,
    expert_out,
    memory_weight,
    decode_inputs,
    self_cache,
    context_lengths,
    old_memory,
    old_lengths,
    slot_of,
    qkv_weight,
    self_out_weight,
    cross_query_weight,
    cross_out_weight,
):
    devices = lax.axis_size("expert")
    own_index = lax.axis_index("expert")
    token_count = source_tokens.shape[0]
    expert_count = router_weight.shape[1]
    planes = devices // EXP_SPLIT
    plane = own_index // EXP_SPLIT
    capacity = 3 * token_count // expert_count
    slot_count = decode_inputs.shape[1]

    hidden_rows = normalized(source_tokens).astype(BF)
    logits = jnp.dot(hidden_rows, router_weight, preferred_element_type=F32)
    one_hot = routes[:, :, None] == jnp.arange(expert_count, dtype=jnp.int32)[None, None, :]
    chosen = jnp.sum(jnp.where(one_hot, logits[:, None, :], 0.0), axis=-1)
    leading = jax.nn.sigmoid(chosen[:, 0] - chosen[:, 1])
    member = jnp.any(one_hot, axis=1)
    earlier = (
        jnp.arange(token_count, dtype=jnp.int32)[:, None] > jnp.arange(token_count, dtype=jnp.int32)[None, :]
    ).astype(BF)
    rank = jnp.dot(earlier, member.astype(BF), preferred_element_type=F32).astype(jnp.int32)
    w_in = expert_in[0]
    w_out = expert_out[0]

    def choice(distance):
        target = (plane + distance) % planes
        is_target = jnp.arange(expert_count, dtype=jnp.int32) == target
        there = jnp.any(member & is_target[None, :], axis=1)
        place = jnp.sum(jnp.where(is_target[None, :], rank, 0), axis=1)
        place = jnp.where(there, place, -1)
        gate = jnp.where(routes[:, 0] == target, leading, 0.0) + jnp.where(
            routes[:, 1] == target, 1.0 - leading, 0.0
        )
        return place, gate

    distances = turn_order(planes) + [0]
    spots = jnp.arange(capacity, dtype=jnp.int32)
    choices = {d: choice(d) for d in distances}

    def picked(distance):
        place, _ = choices[distance]
        pick = (place[None, :] == spots[:, None]).astype(BF)
        return jnp.dot(pick, hidden_rows, preferred_element_type=F32).astype(BF)

    def product(rows):
        return matmul(jnp.maximum(matmul(rows, w_in), 0.0).astype(BF), w_out)

    global_slots = own_index * slot_count + jnp.arange(slot_count, dtype=jnp.int32)
    new_slots = slot_of.reshape(devices, HELD)[:, :SRC_DEV].reshape(-1)
    fresh_slot = jnp.any(global_slots[:, None] == new_slots[None, :], axis=-1)
    effective = jnp.where(fresh_slot, 0, context_lengths)
    cache_mask = (jnp.arange(CTX, dtype=jnp.int32)[None, :] < effective[:, None]).astype(F32)
    cache_keys = self_cache[:, :, :KV].reshape(slot_count, CTX, HEADS, HD)
    cache_values = self_cache[:, :, KV:].reshape(slot_count, CTX, HEADS, HD)
    count = slot_of.shape[0]
    to_request = (slot_of[:, None] == jnp.arange(count, dtype=jnp.int32)[None, :]).astype(BF)

    row = jnp.arange(STEPS * count, dtype=jnp.int32)
    row_place = row // (STEPS * HELD) * HELD + row % HELD
    row_step = row // HELD % STEPS
    slot_from = slot_of[row_place]
    row_from = slot_from // HELD * (STEPS * HELD) + row_step * HELD + slot_from % HELD
    order_request = (row_from[:, None] == row[None, :]).astype(BF)
    order_slot = (row[:, None] == row_from[None, :]).astype(BF)
    steps = jnp.arange(STEPS, dtype=jnp.int32)
    causal = (steps[:, None] >= steps[None, :]).astype(F32)
    key_mask = jnp.concatenate(
        [
            jnp.broadcast_to(cache_mask[:, None, :], (slot_count, STEPS, CTX)),
            jnp.broadcast_to(causal[None], (slot_count, STEPS, STEPS)),
        ],
        axis=2,
    )

    def self_attention(current):
        current = current.astype(BF).reshape(STEPS, slot_count, 3, HEADS, HD).transpose(1, 0, 2, 3, 4)
        all_keys = jnp.concatenate([cache_keys, current[:, :, 1]], axis=1)
        all_values = jnp.concatenate([cache_values, current[:, :, 2]], axis=1)
        attended = jax.vmap(attend_shared)(current[:, :, 0], all_keys, all_values, key_mask)
        return attended.transpose(1, 0, 2, 3).reshape(STEPS * slot_count, KV)

    old_keys = old_memory[:, :, :KV].reshape(OLD_DEV, SRC_MAX, HEADS, HD)
    old_values = old_memory[:, :, KV:].reshape(OLD_DEV, SRC_MAX, HEADS, HD)
    old_mask = (jnp.arange(SRC_MAX, dtype=jnp.int32)[None, :] < old_lengths[:, None]).astype(F32)

    inputs_wide = decode_inputs.astype(F32).reshape(STEPS * slot_count, -1)
    normed_inputs = normalized(decode_inputs).astype(BF).reshape(STEPS * slot_count, -1)

    def query_rows(x):
        return spread_features(normalized(inputs_wide + x).astype(BF))

    decode_stages = [
        lambda x: spread_features(x),
        lambda x: sum_in_plane(matmul(x, qkv_weight), devices, own_index),
        lambda x: sum_planes(x, devices, own_index),
        lambda x: spread_features(self_attention(x)),
        lambda x: sum_in_plane(matmul(x, self_out_weight), devices, own_index),
        lambda x: sum_planes(x, devices, own_index),
        lambda x: query_rows(x),
        lambda x: sum_in_plane(matmul(reorder(order_request, x), cross_query_weight), devices, own_index),
        lambda x: sum_planes(x, devices, own_index),
    ]

    sequence = [0, planes // 2] + [d for d in turn_order(planes) if d != planes // 2]
    last = len(sequence)
    state = {("pick", i): picked(d) for i, d in enumerate(sequence)}
    state[("at", 0)] = state.pop(("pick", 0))
    state["decode"] = normed_inputs
    for phase in range(last + 5):
        keys = sorted(state, key=str)
        state = dict(zip(keys, lax.optimization_barrier(tuple(state[k] for k in keys))))
        made = {}
        for i, distance in enumerate(sequence):
            station = phase - i
            if station == -1:
                made[("at", i)] = turn(state.pop(("pick", i)), devices, distance)
            elif station == 0:
                made[("side", i)] = swap(state[("at", i)], devices, 2)
            elif station == 1:
                rows = jnp.concatenate([state.pop(("at", i)), state.pop(("side", i))], axis=0)
                made[("rows", i)] = rows
                made[("core", i)] = swap(rows, devices, 1)
            elif station == 2:
                partial = product(jnp.concatenate([state.pop(("rows", i)), state.pop(("core", i))], axis=0))
                made[("own", i)] = partial[: 2 * capacity]
                made[("sent", i)] = partial[2 * capacity :].astype(BF)
            elif station == 3:
                made[("sent", i)] = swap(state.pop(("sent", i)), devices, 1)
            elif station == 4:
                half = state.pop(("own", i)) + state.pop(("sent", i)).astype(F32)
                made[("half", i)] = half[:capacity]
                made[("far", i)] = swap(half[capacity:].astype(BF), devices, 2)
            elif station == 5:
                full = (state.pop(("half", i)) + state.pop(("far", i)).astype(F32)).astype(BF)
                made[("back", i)] = turn(full, devices, planes - distance) if distance else full
        stage = phase
        if stage < len(decode_stages):
            state["decode"] = decode_stages[stage](state["decode"])
            if stage == 5:
                made["self_sum"] = state["decode"]
        state.update(made)
    stage = last + 5
    while stage < len(decode_stages):
        state["decode"] = decode_stages[stage](state["decode"])
        stage += 1
    after_self = inputs_wide + state["self_sum"]
    cross_rows = state["decode"].astype(BF).reshape(STEPS, HELD, HEADS, HD)
    back = {d: state[("back", i)] for i, d in enumerate(sequence)}
    old_out = jax.vmap(attend_shared)(
        cross_rows[:, SRC_DEV:].transpose(1, 0, 2, 3),
        old_keys,
        old_values,
        jnp.broadcast_to(old_mask[:, None, :], (OLD_DEV, STEPS, SRC_MAX)),
    ).transpose(1, 0, 2, 3)

    encoder_sum = source_tokens.astype(F32)
    for distance in distances:
        place, gate = choices[distance]
        pick = (place[:, None] == spots[None, :]).astype(BF)
        encoder_sum = encoder_sum + gate[:, None] * jnp.dot(pick, back[distance], preferred_element_type=F32)
    encoded = encoder_sum.astype(BF)
    memory = normalized(encoder_sum).astype(BF)
    memory_kv = jnp.dot(memory, memory_weight, preferred_element_type=F32).astype(BF)
    new_keys = memory_kv[:, :KV].reshape(TOK_DEV, HEADS, HD)
    new_values = memory_kv[:, KV:].reshape(TOK_DEV, HEADS, HD)
    bounds = jnp.cumsum(source_lengths[0])
    segment = jnp.sum(
        (jnp.arange(TOK_DEV, dtype=jnp.int32)[:, None] >= bounds[None, :]).astype(jnp.int32),
        axis=-1,
    )
    new_mask = (segment[None, :] == jnp.arange(SRC_DEV, dtype=jnp.int32)[:, None]).astype(F32)
    new_out = attend_shared(
        cross_rows[:, :SRC_DEV].reshape(STEPS * SRC_DEV, HEADS, HD),
        new_keys,
        new_values,
        jnp.tile(new_mask, (STEPS, 1)),
    ).reshape(STEPS, SRC_DEV, HEADS, HD)
    held_out = jnp.concatenate([new_out, old_out], axis=1).reshape(STEPS * HELD, KV)
    cross_rows_out = reorder(order_slot, spread_features(held_out))
    cross_sum = sum_planes(
        sum_in_plane(matmul(cross_rows_out, cross_out_weight), devices, own_index), devices, own_index
    )
    decoded = (after_self + cross_sum).astype(BF).reshape(STEPS, slot_count, -1)
    return (encoded, decoded)


def solution(mesh):
    return jax.shard_map(
        body,
        mesh=mesh,
        in_specs=(
            P(("group", "expert"), None),
            P(("group", "expert"), None),
            P(("group", "expert"), None),
            P(),
            P("expert", None, None),
            P("expert", None, None),
            P(),
            P(None, ("group", "expert"), None),
            P(("group", "expert"), None, None),
            P(("group", "expert")),
            P(("group", "expert"), None, None),
            P(("group", "expert")),
            P("group"),
            P("expert", None),
            P("expert", None),
            P("expert", None),
            P("expert", None),
        ),
        out_specs=(P(("group", "expert"), None), P(None, ("group", "expert"), None)),
        check_vma=False,
    )
```

```python
import jax
import jax.numpy as jnp
from jax import lax
from jax.sharding import PartitionSpec as P

HEADS = 8
HD = 128
EXP_SPLIT = 4
SRC_DEV = 4
OLD_DEV = 2
TOK_DEV = 256
CTX = 64
KV = 1024
SRC_MAX = 192
HELD = 6
STEPS = 2
BF = jnp.bfloat16
F32 = jnp.float32


def normalized(values):
    values = values.astype(jnp.float32)
    average = jnp.mean(values, axis=-1, keepdims=True)
    centred = values - average
    variance = jnp.mean(centred * centred, axis=-1, keepdims=True)
    return centred * lax.rsqrt(variance + 1e-05)


def attend_shared(queries, all_keys, all_values, key_mask):
    scores = jnp.einsum("phd,jhd->phj", queries, all_keys, preferred_element_type=F32) * HD ** (-0.5)
    raised = jnp.exp(scores) * key_mask[:, None, :]
    weights_bf = (raised / jnp.sum(raised, axis=-1, keepdims=True)).astype(BF)
    result = jnp.einsum("phj,jhd->phd", weights_bf, all_values, preferred_element_type=F32)
    return result.astype(BF)


def swap(values, devices, bit):
    return lax.ppermute(values, "expert", [(i, i ^ bit) for i in range(devices)])


def turn(values, devices, distance):
    step = EXP_SPLIT * distance
    return lax.ppermute(values, "expert", [(i, (i + step) % devices) for i in range(devices)])


def turn_order(planes):
    order = []
    for distance in range(1, planes // 2 + 1):
        order.append(distance)
        if planes - distance != distance:
            order.append(planes - distance)
    return order


def rows_at(values, index, count):
    return lax.dynamic_slice_in_dim(values, index * count, count, 0)


def sum_in_plane(partial, devices, own_index):
    core = own_index % 2
    side = (own_index // 2) % 2
    count = partial.shape[0] // 2
    sent = rows_at(partial, 1 - core, count).astype(BF)
    kept = rows_at(partial, core, count) + swap(sent, devices, 1).astype(F32)
    count = count // 2
    sent = rows_at(kept, 1 - side, count).astype(BF)
    return rows_at(kept, side, count) + swap(sent, devices, 2).astype(F32)


def sum_planes(kept, devices, own_index):
    planes = devices // EXP_SPLIT
    plane = own_index // EXP_SPLIT
    count = kept.shape[0] // planes
    total = rows_at(kept, plane, count)
    low = kept.astype(BF)
    for distance in turn_order(planes):
        total = total + turn(rows_at(low, (plane + distance) % planes, count), devices, distance).astype(F32)
    return total


def spread_features(local_rows):
    return lax.all_to_all(local_rows, "expert", split_axis=1, concat_axis=0, tiled=True)


def reorder(order, spread):
    return jnp.dot(order, spread, preferred_element_type=F32).astype(BF)


def matmul(left, right):
    return jnp.dot(left, right, preferred_element_type=F32)


def body(
    source_tokens,
    routes,
    source_lengths,
    router_weight,
    expert_in,
    expert_out,
    memory_weight,
    decode_inputs,
    self_cache,
    context_lengths,
    old_memory,
    old_lengths,
    slot_of,
    qkv_weight,
    self_out_weight,
    cross_query_weight,
    cross_out_weight,
):
    devices = lax.axis_size("expert")
    own_index = lax.axis_index("expert")
    token_count = source_tokens.shape[0]
    expert_count = router_weight.shape[1]
    planes = devices // EXP_SPLIT
    plane = own_index // EXP_SPLIT
    capacity = 3 * token_count // expert_count
    slot_count = decode_inputs.shape[1]

    hidden_rows = normalized(source_tokens).astype(BF)
    logits = jnp.dot(hidden_rows, router_weight, preferred_element_type=F32)
    one_hot = routes[:, :, None] == jnp.arange(expert_count, dtype=jnp.int32)[None, None, :]
    chosen = jnp.sum(jnp.where(one_hot, logits[:, None, :], 0.0), axis=-1)
    leading = jax.nn.sigmoid(chosen[:, 0] - chosen[:, 1])
    member = jnp.any(one_hot, axis=1)
    earlier = (
        jnp.arange(token_count, dtype=jnp.int32)[:, None] > jnp.arange(token_count, dtype=jnp.int32)[None, :]
    ).astype(BF)
    rank = jnp.dot(earlier, member.astype(BF), preferred_element_type=F32).astype(jnp.int32)
    w_in = expert_in[0]
    w_out = expert_out[0]

    def choice(distance):
        target = (plane + distance) % planes
        is_target = jnp.arange(expert_count, dtype=jnp.int32) == target
        there = jnp.any(member & is_target[None, :], axis=1)
        place = jnp.sum(jnp.where(is_target[None, :], rank, 0), axis=1)
        place = jnp.where(there, place, -1)
        gate = jnp.where(routes[:, 0] == target, leading, 0.0) + jnp.where(
            routes[:, 1] == target, 1.0 - leading, 0.0
        )
        return place, gate

    distances = turn_order(planes) + [0]
    spots = jnp.arange(capacity, dtype=jnp.int32)
    choices = {d: choice(d) for d in distances}

    def picked(distance):
        place, _ = choices[distance]
        pick = (place[None, :] == spots[:, None]).astype(BF)
        return jnp.dot(pick, hidden_rows, preferred_element_type=F32).astype(BF)

    def product(rows):
        return matmul(jnp.maximum(matmul(rows, w_in), 0.0).astype(BF), w_out)

    global_slots = own_index * slot_count + jnp.arange(slot_count, dtype=jnp.int32)
    new_slots = slot_of.reshape(devices, HELD)[:, :SRC_DEV].reshape(-1)
    fresh_slot = jnp.any(global_slots[:, None] == new_slots[None, :], axis=-1)
    effective = jnp.where(fresh_slot, 0, context_lengths)
    cache_mask = (jnp.arange(CTX, dtype=jnp.int32)[None, :] < effective[:, None]).astype(F32)
    cache_keys = self_cache[:, :, :KV].reshape(slot_count, CTX, HEADS, HD)
    cache_values = self_cache[:, :, KV:].reshape(slot_count, CTX, HEADS, HD)
    count = slot_of.shape[0]
    to_request = (slot_of[:, None] == jnp.arange(count, dtype=jnp.int32)[None, :]).astype(BF)

    row = jnp.arange(STEPS * count, dtype=jnp.int32)
    held = STEPS * HELD
    target = row // held
    target_device = target % planes * EXP_SPLIT + target // planes % 2 * 2 + target // (2 * planes)
    target_row = target_device * held + row % held

    def source_of(rows):
        slots = slot_of[rows // held * HELD + rows % HELD]
        return slots // HELD * held + rows // HELD % STEPS * HELD + slots % HELD

    order_plain = (target_row[:, None] == row[None, :]).astype(BF)
    order_request = (source_of(target_row)[:, None] == row[None, :]).astype(BF)
    order_slot = (target_row[:, None] == source_of(row)[None, :]).astype(BF)
    steps = jnp.arange(STEPS, dtype=jnp.int32)
    causal = (steps[:, None] >= steps[None, :]).astype(F32)
    key_mask = jnp.concatenate(
        [
            jnp.broadcast_to(cache_mask[:, None, :], (slot_count, STEPS, CTX)),
            jnp.broadcast_to(causal[None], (slot_count, STEPS, STEPS)),
        ],
        axis=2,
    )

    def self_attention(current):
        current = current.astype(BF).reshape(STEPS, slot_count, 3, HEADS, HD).transpose(1, 0, 2, 3, 4)
        all_keys = jnp.concatenate([cache_keys, current[:, :, 1]], axis=1)
        all_values = jnp.concatenate([cache_values, current[:, :, 2]], axis=1)
        attended = jax.vmap(attend_shared)(current[:, :, 0], all_keys, all_values, key_mask)
        return attended.transpose(1, 0, 2, 3).reshape(STEPS * slot_count, KV)

    old_keys = old_memory[:, :, :KV].reshape(OLD_DEV, SRC_MAX, HEADS, HD)
    old_values = old_memory[:, :, KV:].reshape(OLD_DEV, SRC_MAX, HEADS, HD)
    old_mask = (jnp.arange(SRC_MAX, dtype=jnp.int32)[None, :] < old_lengths[:, None]).astype(F32)

    inputs_wide = decode_inputs.astype(F32).reshape(STEPS * slot_count, -1)
    normed_inputs = normalized(decode_inputs).astype(BF).reshape(STEPS * slot_count, -1)

    def query_rows(x):
        return spread_features(normalized(inputs_wide + x).astype(BF))

    decode_stages = [
        lambda x: spread_features(x),
        lambda x: sum_in_plane(matmul(reorder(order_plain, x), qkv_weight), devices, own_index),
        lambda x: sum_planes(x, devices, own_index),
        lambda x: spread_features(self_attention(x)),
        lambda x: sum_in_plane(matmul(reorder(order_plain, x), self_out_weight), devices, own_index),
        lambda x: sum_planes(x, devices, own_index),
        lambda x: query_rows(x),
        lambda x: sum_in_plane(matmul(reorder(order_request, x), cross_query_weight), devices, own_index),
        lambda x: sum_planes(x, devices, own_index),
    ]

    sequence = [0, planes // 2] + [d for d in turn_order(planes) if d != planes // 2]
    last = len(sequence)
    state = {("pick", i): picked(sequence[i]) for i in range(2)}
    state[("at", 0)] = state.pop(("pick", 0))
    state["decode"] = decode_stages[0](normed_inputs)
    stage = 1
    for phase in range(last + 5):
        keys = sorted(state, key=str)
        state = dict(zip(keys, lax.optimization_barrier(tuple(state[k] for k in keys))))
        made = {}
        for i, distance in enumerate(sequence):
            station = phase - i
            if station == -2 and i > 1 or phase == 0 and i > 2:
                made[("pick", i)] = picked(distance)
            if station == -1:
                made[("at", i)] = turn(state.pop(("pick", i)), devices, distance)
            elif station == 0:
                made[("side", i)] = swap(state[("at", i)], devices, 2)
            elif station == 1:
                made[("core", i)] = swap(state[("at", i)], devices, 1)
                made[("diagonal", i)] = swap(state[("side", i)], devices, 1)
            elif station == 2:
                partial = product(
                    jnp.concatenate([state.pop((k, i)) for k in ("at", "side", "core", "diagonal")], axis=0)
                )
                made[("own", i)] = partial[: 2 * capacity]
                made[("sent", i)] = partial[2 * capacity :].astype(BF)
            elif station == 3:
                made[("sent", i)] = swap(state.pop(("sent", i)), devices, 1)
            elif station == 4:
                half = state.pop(("own", i)) + state.pop(("sent", i)).astype(F32)
                made[("half", i)] = half[:capacity]
                made[("far", i)] = swap(half[capacity:].astype(BF), devices, 2)
            elif station == 5:
                full = (state.pop(("half", i)) + state.pop(("far", i)).astype(F32)).astype(BF)
                made[("back", i)] = turn(full, devices, planes - distance) if distance else full
        for _ in range(1 if phase else 2):
            if stage < len(decode_stages):
                state["decode"] = decode_stages[stage](state["decode"])
                if stage == 5:
                    made["self_sum"] = state["decode"]
                stage += 1
        state.update(made)
    while stage < len(decode_stages):
        state["decode"] = decode_stages[stage](state["decode"])
        stage += 1
    after_self = inputs_wide + state["self_sum"]
    cross_rows = state["decode"].astype(BF).reshape(STEPS, HELD, HEADS, HD)
    back = {d: state[("back", i)] for i, d in enumerate(sequence)}
    old_out = jax.vmap(attend_shared)(
        cross_rows[:, SRC_DEV:].transpose(1, 0, 2, 3),
        old_keys,
        old_values,
        jnp.broadcast_to(old_mask[:, None, :], (OLD_DEV, STEPS, SRC_MAX)),
    ).transpose(1, 0, 2, 3)

    encoder_sum = source_tokens.astype(F32)
    for distance in distances:
        place, gate = choices[distance]
        pick = (place[:, None] == spots[None, :]).astype(BF)
        encoder_sum = encoder_sum + gate[:, None] * jnp.dot(pick, back[distance], preferred_element_type=F32)
    encoded = encoder_sum.astype(BF)
    memory = normalized(encoder_sum).astype(BF)
    memory_kv = jnp.dot(memory, memory_weight, preferred_element_type=F32).astype(BF)
    new_keys = memory_kv[:, :KV].reshape(TOK_DEV, HEADS, HD)
    new_values = memory_kv[:, KV:].reshape(TOK_DEV, HEADS, HD)
    bounds = jnp.cumsum(source_lengths[0])
    segment = jnp.sum(
        (jnp.arange(TOK_DEV, dtype=jnp.int32)[:, None] >= bounds[None, :]).astype(jnp.int32),
        axis=-1,
    )
    new_mask = (segment[None, :] == jnp.arange(SRC_DEV, dtype=jnp.int32)[:, None]).astype(F32)
    new_out = attend_shared(
        cross_rows[:, :SRC_DEV].reshape(STEPS * SRC_DEV, HEADS, HD),
        new_keys,
        new_values,
        jnp.tile(new_mask, (STEPS, 1)),
    ).reshape(STEPS, SRC_DEV, HEADS, HD)
    held_out = jnp.concatenate([new_out, old_out], axis=1).reshape(STEPS * HELD, KV)
    cross_rows_out = reorder(order_slot, spread_features(held_out))
    cross_sum = sum_planes(
        sum_in_plane(matmul(cross_rows_out, cross_out_weight), devices, own_index), devices, own_index
    )
    decoded = (after_self + cross_sum).astype(BF).reshape(STEPS, slot_count, -1)
    return (encoded, decoded)


def solution(mesh):
    return jax.shard_map(
        body,
        mesh=mesh,
        in_specs=(
            P(("group", "expert"), None),
            P(("group", "expert"), None),
            P(("group", "expert"), None),
            P(),
            P("expert", None, None),
            P("expert", None, None),
            P(),
            P(None, ("group", "expert"), None),
            P(("group", "expert"), None, None),
            P(("group", "expert")),
            P(("group", "expert"), None, None),
            P(("group", "expert")),
            P("group"),
            P("expert", None),
            P("expert", None),
            P("expert", None),
            P("expert", None),
        ),
        out_specs=(P(("group", "expert"), None), P(None, ("group", "expert"), None)),
        check_vma=False,
    )
```

```python
import jax
import jax.numpy as jnp
from jax import lax
from jax.sharding import PartitionSpec as P

HEADS = 8
HD = 128
EXP_SPLIT = 4
SRC_DEV = 4
OLD_DEV = 2
TOK_DEV = 256
CTX = 64
KV = 1024
SRC_MAX = 192
HELD = 6
STEPS = 2
BF = jnp.bfloat16
F32 = jnp.float32


def normalized(values):
    values = values.astype(jnp.float32)
    average = jnp.mean(values, axis=-1, keepdims=True)
    centred = values - average
    variance = jnp.mean(centred * centred, axis=-1, keepdims=True)
    return centred * lax.rsqrt(variance + 1e-05)


def attend_shared(queries, all_keys, all_values, key_mask):
    scores = jnp.einsum("phd,jhd->phj", queries, all_keys, preferred_element_type=F32) * HD ** (-0.5)
    raised = jnp.exp(scores) * key_mask[:, None, :]
    weights_bf = (raised / jnp.sum(raised, axis=-1, keepdims=True)).astype(BF)
    result = jnp.einsum("phj,jhd->phd", weights_bf, all_values, preferred_element_type=F32)
    return result.astype(BF)


def swap(values, devices, bit):
    return lax.ppermute(values, "expert", [(i, i ^ bit) for i in range(devices)])


def turn(values, devices, distance):
    step = EXP_SPLIT * distance
    return lax.ppermute(values, "expert", [(i, (i + step) % devices) for i in range(devices)])


def turn_order(planes):
    order = []
    for distance in range(1, planes // 2 + 1):
        order.append(distance)
        if planes - distance != distance:
            order.append(planes - distance)
    return order


def rows_at(values, index, count):
    return lax.dynamic_slice_in_dim(values, index * count, count, 0)


def sum_in_plane(partial, devices, own_index):
    core = own_index % 2
    side = (own_index // 2) % 2
    count = partial.shape[0] // 2
    sent = rows_at(partial, 1 - core, count).astype(BF)
    kept = rows_at(partial, core, count) + swap(sent, devices, 1).astype(F32)
    count = count // 2
    sent = rows_at(kept, 1 - side, count).astype(BF)
    return rows_at(kept, side, count) + swap(sent, devices, 2).astype(F32)


def sum_planes(kept, devices, own_index):
    planes = devices // EXP_SPLIT
    plane = own_index // EXP_SPLIT
    count = kept.shape[0] // planes
    total = rows_at(kept, plane, count)
    low = kept.astype(BF)
    for distance in turn_order(planes):
        total = total + turn(rows_at(low, (plane + distance) % planes, count), devices, distance).astype(F32)
    return total


def sum_lines(kept, devices):
    planes = devices // EXP_SPLIT
    lines = [[plane * EXP_SPLIT + place for plane in range(planes)] for place in range(EXP_SPLIT)]
    parts = lax.all_to_all(
        kept.astype(BF), "expert", split_axis=0, concat_axis=0, tiled=True, axis_index_groups=lines
    )
    return jnp.sum(parts.reshape(planes, -1, kept.shape[1]).astype(F32), axis=0)


def spread_features(local_rows):
    return lax.all_to_all(local_rows, "expert", split_axis=1, concat_axis=0, tiled=True)


def reorder(order, spread):
    return jnp.dot(order, spread, preferred_element_type=F32).astype(BF)


def matmul(left, right):
    return jnp.dot(left, right, preferred_element_type=F32)


def body(
    source_tokens,
    routes,
    source_lengths,
    router_weight,
    expert_in,
    expert_out,
    memory_weight,
    decode_inputs,
    self_cache,
    context_lengths,
    old_memory,
    old_lengths,
    slot_of,
    qkv_weight,
    self_out_weight,
    cross_query_weight,
    cross_out_weight,
):
    devices = lax.axis_size("expert")
    own_index = lax.axis_index("expert")
    token_count = source_tokens.shape[0]
    expert_count = router_weight.shape[1]
    planes = devices // EXP_SPLIT
    plane = own_index // EXP_SPLIT
    capacity = 3 * token_count // expert_count
    slot_count = decode_inputs.shape[1]

    hidden_rows = normalized(source_tokens).astype(BF)
    logits = jnp.dot(hidden_rows, router_weight, preferred_element_type=F32)
    one_hot = routes[:, :, None] == jnp.arange(expert_count, dtype=jnp.int32)[None, None, :]
    chosen = jnp.sum(jnp.where(one_hot, logits[:, None, :], 0.0), axis=-1)
    leading = jax.nn.sigmoid(chosen[:, 0] - chosen[:, 1])
    member = jnp.any(one_hot, axis=1)
    earlier = (
        jnp.arange(token_count, dtype=jnp.int32)[:, None] > jnp.arange(token_count, dtype=jnp.int32)[None, :]
    ).astype(BF)
    rank = jnp.dot(earlier, member.astype(BF), preferred_element_type=F32).astype(jnp.int32)
    w_in = expert_in[0]
    w_out = expert_out[0]

    def choice(distance):
        target = (plane + distance) % planes
        is_target = jnp.arange(expert_count, dtype=jnp.int32) == target
        there = jnp.any(member & is_target[None, :], axis=1)
        place = jnp.sum(jnp.where(is_target[None, :], rank, 0), axis=1)
        place = jnp.where(there, place, -1)
        gate = jnp.where(routes[:, 0] == target, leading, 0.0) + jnp.where(
            routes[:, 1] == target, 1.0 - leading, 0.0
        )
        return place, gate

    distances = turn_order(planes) + [0]
    spots = jnp.arange(capacity, dtype=jnp.int32)
    choices = {d: choice(d) for d in distances}

    def picked(distance):
        place, _ = choices[distance]
        pick = (place[None, :] == spots[:, None]).astype(BF)
        return jnp.dot(pick, hidden_rows, preferred_element_type=F32).astype(BF)

    def product(rows):
        return matmul(jnp.maximum(matmul(rows, w_in), 0.0).astype(BF), w_out)

    global_slots = own_index * slot_count + jnp.arange(slot_count, dtype=jnp.int32)
    new_slots = slot_of.reshape(devices, HELD)[:, :SRC_DEV].reshape(-1)
    fresh_slot = jnp.any(global_slots[:, None] == new_slots[None, :], axis=-1)
    effective = jnp.where(fresh_slot, 0, context_lengths)
    cache_mask = (jnp.arange(CTX, dtype=jnp.int32)[None, :] < effective[:, None]).astype(F32)
    cache_keys = self_cache[:, :, :KV].reshape(slot_count, CTX, HEADS, HD)
    cache_values = self_cache[:, :, KV:].reshape(slot_count, CTX, HEADS, HD)
    count = slot_of.shape[0]
    to_request = (slot_of[:, None] == jnp.arange(count, dtype=jnp.int32)[None, :]).astype(BF)

    row = jnp.arange(STEPS * count, dtype=jnp.int32)
    held = STEPS * HELD
    target = row // held
    target_device = target % planes * EXP_SPLIT + target // planes % 2 * 2 + target // (2 * planes)
    target_row = target_device * held + row % held

    def source_of(rows):
        slots = slot_of[rows // held * HELD + rows % HELD]
        return slots // HELD * held + rows // HELD % STEPS * HELD + slots % HELD

    order_plain = (target_row[:, None] == row[None, :]).astype(BF)
    order_request = (source_of(target_row)[:, None] == row[None, :]).astype(BF)
    order_slot = (target_row[:, None] == source_of(row)[None, :]).astype(BF)
    steps = jnp.arange(STEPS, dtype=jnp.int32)
    causal = (steps[:, None] >= steps[None, :]).astype(F32)
    key_mask = jnp.concatenate(
        [
            jnp.broadcast_to(cache_mask[:, None, :], (slot_count, STEPS, CTX)),
            jnp.broadcast_to(causal[None], (slot_count, STEPS, STEPS)),
        ],
        axis=2,
    )

    def self_attention(current):
        current = current.astype(BF).reshape(STEPS, slot_count, 3, HEADS, HD).transpose(1, 0, 2, 3, 4)
        all_keys = jnp.concatenate([cache_keys, current[:, :, 1]], axis=1)
        all_values = jnp.concatenate([cache_values, current[:, :, 2]], axis=1)
        attended = jax.vmap(attend_shared)(current[:, :, 0], all_keys, all_values, key_mask)
        return attended.transpose(1, 0, 2, 3).reshape(STEPS * slot_count, KV)

    old_keys = old_memory[:, :, :KV].reshape(OLD_DEV, SRC_MAX, HEADS, HD)
    old_values = old_memory[:, :, KV:].reshape(OLD_DEV, SRC_MAX, HEADS, HD)
    old_mask = (jnp.arange(SRC_MAX, dtype=jnp.int32)[None, :] < old_lengths[:, None]).astype(F32)

    inputs_wide = decode_inputs.astype(F32).reshape(STEPS * slot_count, -1)
    normed_inputs = normalized(decode_inputs).astype(BF).reshape(STEPS * slot_count, -1)

    def query_rows(x):
        return spread_features(normalized(inputs_wide + x).astype(BF))

    decode_stages = [
        lambda x: spread_features(x),
        lambda x: sum_in_plane(matmul(reorder(order_plain, x), qkv_weight), devices, own_index),
        lambda x: sum_planes(x, devices, own_index),
        lambda x: spread_features(self_attention(x)),
        lambda x: sum_in_plane(matmul(reorder(order_plain, x), self_out_weight), devices, own_index),
        lambda x: sum_lines(x, devices),
        lambda x: query_rows(x),
        lambda x: sum_in_plane(matmul(reorder(order_request, x), cross_query_weight), devices, own_index),
        lambda x: sum_planes(x, devices, own_index),
    ]

    sequence = [0, planes // 2] + [d for d in turn_order(planes) if d != planes // 2]
    last = len(sequence)
    state = {("pick", i): picked(sequence[i]) for i in range(2)}
    state[("at", 0)] = state.pop(("pick", 0))
    state["decode"] = decode_stages[0](normed_inputs)
    stages_of = {0: (1, 2), 1: (3,), 2: (4,), 3: (5,), 4: (6,), 6: (7,), 7: (8,)}
    for phase in range(last + 5):
        keys = sorted(state, key=str)
        state = dict(zip(keys, lax.optimization_barrier(tuple(state[k] for k in keys))))
        made = {}
        for i, distance in enumerate(sequence):
            station = phase - i
            if station == -2 and i > 1 or phase == 0 and i > 2:
                made[("pick", i)] = picked(distance)
            if station == -1:
                made[("at", i)] = turn(state.pop(("pick", i)), devices, distance)
            elif station == 0:
                made[("side", i)] = swap(state[("at", i)], devices, 2)
            elif station == 1:
                made[("core", i)] = swap(state[("at", i)], devices, 1)
                made[("diagonal", i)] = swap(state[("side", i)], devices, 1)
            elif station == 2:
                partial = product(
                    jnp.concatenate([state.pop((k, i)) for k in ("at", "side", "core", "diagonal")], axis=0)
                )
                made[("own", i)] = partial[: 2 * capacity]
                made[("sent", i)] = partial[2 * capacity :].astype(BF)
            elif station == 3:
                made[("sent", i)] = swap(state.pop(("sent", i)), devices, 1)
            elif station == 4:
                half = state.pop(("own", i)) + state.pop(("sent", i)).astype(F32)
                made[("half", i)] = half[:capacity]
                made[("far", i)] = swap(half[capacity:].astype(BF), devices, 2)
            elif station == 5:
                full = (state.pop(("half", i)) + state.pop(("far", i)).astype(F32)).astype(BF)
                made[("back", i)] = turn(full, devices, planes - distance) if distance else full
        for stage in stages_of.get(phase, ()):
            state["decode"] = decode_stages[stage](state["decode"])
            if stage == 5:
                made["self_sum"] = state["decode"]
        state.update(made)
    after_self = inputs_wide + state["self_sum"]
    cross_rows = state["decode"].astype(BF).reshape(STEPS, HELD, HEADS, HD)
    back = {d: state[("back", i)] for i, d in enumerate(sequence)}
    old_out = jax.vmap(attend_shared)(
        cross_rows[:, SRC_DEV:].transpose(1, 0, 2, 3),
        old_keys,
        old_values,
        jnp.broadcast_to(old_mask[:, None, :], (OLD_DEV, STEPS, SRC_MAX)),
    ).transpose(1, 0, 2, 3)

    encoder_sum = source_tokens.astype(F32)
    for distance in distances:
        place, gate = choices[distance]
        pick = (place[:, None] == spots[None, :]).astype(BF)
        encoder_sum = encoder_sum + gate[:, None] * jnp.dot(pick, back[distance], preferred_element_type=F32)
    encoded = encoder_sum.astype(BF)
    memory = normalized(encoder_sum).astype(BF)
    memory_kv = jnp.dot(memory, memory_weight, preferred_element_type=F32).astype(BF)
    new_keys = memory_kv[:, :KV].reshape(TOK_DEV, HEADS, HD)
    new_values = memory_kv[:, KV:].reshape(TOK_DEV, HEADS, HD)
    bounds = jnp.cumsum(source_lengths[0])
    segment = jnp.sum(
        (jnp.arange(TOK_DEV, dtype=jnp.int32)[:, None] >= bounds[None, :]).astype(jnp.int32),
        axis=-1,
    )
    new_mask = (segment[None, :] == jnp.arange(SRC_DEV, dtype=jnp.int32)[:, None]).astype(F32)
    new_out = attend_shared(
        cross_rows[:, :SRC_DEV].reshape(STEPS * SRC_DEV, HEADS, HD),
        new_keys,
        new_values,
        jnp.tile(new_mask, (STEPS, 1)),
    ).reshape(STEPS, SRC_DEV, HEADS, HD)
    held_out = jnp.concatenate([new_out, old_out], axis=1).reshape(STEPS * HELD, KV)
    cross_rows_out = reorder(order_slot, spread_features(held_out))
    cross_sum = sum_planes(
        sum_in_plane(matmul(cross_rows_out, cross_out_weight), devices, own_index), devices, own_index
    )
    decoded = (after_self + cross_sum).astype(BF).reshape(STEPS, slot_count, -1)
    return (encoded, decoded)


def solution(mesh):
    return jax.shard_map(
        body,
        mesh=mesh,
        in_specs=(
            P(("group", "expert"), None),
            P(("group", "expert"), None),
            P(("group", "expert"), None),
            P(),
            P("expert", None, None),
            P("expert", None, None),
            P(),
            P(None, ("group", "expert"), None),
            P(("group", "expert"), None, None),
            P(("group", "expert")),
            P(("group", "expert"), None, None),
            P(("group", "expert")),
            P("group"),
            P("expert", None),
            P("expert", None),
            P("expert", None),
            P("expert", None),
        ),
        out_specs=(P(("group", "expert"), None), P(None, ("group", "expert"), None)),
        check_vma=False,
    )
```

```python
import jax
import jax.numpy as jnp
from jax import lax
from jax.sharding import PartitionSpec as P

HEADS = 8
HD = 128
EXP_SPLIT = 4
SRC_DEV = 4
OLD_DEV = 2
TOK_DEV = 256
CTX = 64
KV = 1024
SRC_MAX = 192
HELD = 6
STEPS = 2
BF = jnp.bfloat16
F32 = jnp.float32


def normalized(values):
    values = values.astype(jnp.float32)
    average = jnp.mean(values, axis=-1, keepdims=True)
    centred = values - average
    variance = jnp.mean(centred * centred, axis=-1, keepdims=True)
    return centred * lax.rsqrt(variance + 1e-05)


def attend_shared(queries, all_keys, all_values, key_mask):
    scores = jnp.einsum("phd,jhd->phj", queries, all_keys, preferred_element_type=F32) * HD ** (-0.5)
    raised = jnp.exp(scores) * key_mask[:, None, :]
    weights_bf = (raised / jnp.sum(raised, axis=-1, keepdims=True)).astype(BF)
    result = jnp.einsum("phj,jhd->phd", weights_bf, all_values, preferred_element_type=F32)
    return result.astype(BF)


def swap(values, devices, bit):
    return lax.ppermute(values, "expert", [(i, i ^ bit) for i in range(devices)])


def turn(values, devices, distance):
    step = EXP_SPLIT * distance
    return lax.ppermute(values, "expert", [(i, (i + step) % devices) for i in range(devices)])


def turn_order(planes):
    order = []
    for distance in range(1, planes // 2 + 1):
        order.append(distance)
        if planes - distance != distance:
            order.append(planes - distance)
    return order


def rows_at(values, index, count):
    return lax.dynamic_slice_in_dim(values, index * count, count, 0)


def sum_in_plane(partial, devices, own_index):
    core = own_index % 2
    side = (own_index // 2) % 2
    count = partial.shape[0] // 2
    sent = rows_at(partial, 1 - core, count).astype(BF)
    kept = rows_at(partial, core, count) + swap(sent, devices, 1).astype(F32)
    count = count // 2
    sent = rows_at(kept, 1 - side, count).astype(BF)
    return rows_at(kept, side, count) + swap(sent, devices, 2).astype(F32)


def sum_planes(kept, devices, own_index):
    planes = devices // EXP_SPLIT
    plane = own_index // EXP_SPLIT
    count = kept.shape[0] // planes
    total = rows_at(kept, plane, count)
    low = kept.astype(BF)
    for distance in turn_order(planes):
        total = total + turn(rows_at(low, (plane + distance) % planes, count), devices, distance).astype(F32)
    return total


def sum_lines(kept, devices):
    planes = devices // EXP_SPLIT
    lines = [[plane * EXP_SPLIT + place for plane in range(planes)] for place in range(EXP_SPLIT)]
    parts = lax.all_to_all(
        kept.astype(BF), "expert", split_axis=0, concat_axis=0, tiled=True, axis_index_groups=lines
    )
    return jnp.sum(parts.reshape(planes, -1, kept.shape[1]).astype(F32), axis=0)


def spread_features(local_rows):
    return lax.all_to_all(local_rows, "expert", split_axis=1, concat_axis=0, tiled=True)


def reorder(order, spread):
    return jnp.dot(order, spread, preferred_element_type=F32).astype(BF)


def matmul(left, right):
    return jnp.dot(left, right, preferred_element_type=F32)


def body(
    source_tokens,
    routes,
    source_lengths,
    router_weight,
    expert_in,
    expert_out,
    memory_weight,
    decode_inputs,
    self_cache,
    context_lengths,
    old_memory,
    old_lengths,
    slot_of,
    qkv_weight,
    self_out_weight,
    cross_query_weight,
    cross_out_weight,
):
    devices = lax.axis_size("expert")
    own_index = lax.axis_index("expert")
    token_count = source_tokens.shape[0]
    expert_count = router_weight.shape[1]
    planes = devices // EXP_SPLIT
    plane = own_index // EXP_SPLIT
    capacity = 3 * token_count // expert_count
    slot_count = decode_inputs.shape[1]

    hidden_rows = normalized(source_tokens).astype(BF)
    logits = jnp.dot(hidden_rows, router_weight, preferred_element_type=F32)
    one_hot = routes[:, :, None] == jnp.arange(expert_count, dtype=jnp.int32)[None, None, :]
    chosen = jnp.sum(jnp.where(one_hot, logits[:, None, :], 0.0), axis=-1)
    leading = jax.nn.sigmoid(chosen[:, 0] - chosen[:, 1])
    member = jnp.any(one_hot, axis=1)
    earlier = (
        jnp.arange(token_count, dtype=jnp.int32)[:, None] > jnp.arange(token_count, dtype=jnp.int32)[None, :]
    ).astype(BF)
    rank = jnp.dot(earlier, member.astype(BF), preferred_element_type=F32).astype(jnp.int32)
    w_in = expert_in[0]
    w_out = expert_out[0]

    def choice(distance):
        target = (plane + distance) % planes
        is_target = jnp.arange(expert_count, dtype=jnp.int32) == target
        there = jnp.any(member & is_target[None, :], axis=1)
        place = jnp.sum(jnp.where(is_target[None, :], rank, 0), axis=1)
        place = jnp.where(there, place, -1)
        gate = jnp.where(routes[:, 0] == target, leading, 0.0) + jnp.where(
            routes[:, 1] == target, 1.0 - leading, 0.0
        )
        return place, gate

    distances = turn_order(planes) + [0]
    spots = jnp.arange(capacity, dtype=jnp.int32)
    choices = {d: choice(d) for d in distances}

    def picked(distance):
        place, _ = choices[distance]
        pick = (place[None, :] == spots[:, None]).astype(BF)
        return jnp.dot(pick, hidden_rows, preferred_element_type=F32).astype(BF)

    def product(rows):
        return matmul(jnp.maximum(matmul(rows, w_in), 0.0).astype(BF), w_out)

    global_slots = own_index * slot_count + jnp.arange(slot_count, dtype=jnp.int32)
    new_slots = slot_of.reshape(devices, HELD)[:, :SRC_DEV].reshape(-1)
    fresh_slot = jnp.any(global_slots[:, None] == new_slots[None, :], axis=-1)
    effective = jnp.where(fresh_slot, 0, context_lengths)
    cache_mask = (jnp.arange(CTX, dtype=jnp.int32)[None, :] < effective[:, None]).astype(F32)
    cache_keys = self_cache[:, :, :KV].reshape(slot_count, CTX, HEADS, HD)
    cache_values = self_cache[:, :, KV:].reshape(slot_count, CTX, HEADS, HD)
    count = slot_of.shape[0]
    to_request = (slot_of[:, None] == jnp.arange(count, dtype=jnp.int32)[None, :]).astype(BF)

    row = jnp.arange(STEPS * count, dtype=jnp.int32)
    held = STEPS * HELD
    target = row // held
    target_device = target % planes * EXP_SPLIT + target // planes % 2 * 2 + target // (2 * planes)
    target_row = target_device * held + row % held

    def source_of(rows):
        slots = slot_of[rows // held * HELD + rows % HELD]
        return slots // HELD * held + rows // HELD % STEPS * HELD + slots % HELD

    order_plain = (target_row[:, None] == row[None, :]).astype(BF)
    order_request = (source_of(target_row)[:, None] == row[None, :]).astype(BF)
    order_slot = (target_row[:, None] == source_of(row)[None, :]).astype(BF)
    steps = jnp.arange(STEPS, dtype=jnp.int32)
    causal = (steps[:, None] >= steps[None, :]).astype(F32)
    key_mask = jnp.concatenate(
        [
            jnp.broadcast_to(cache_mask[:, None, :], (slot_count, STEPS, CTX)),
            jnp.broadcast_to(causal[None], (slot_count, STEPS, STEPS)),
        ],
        axis=2,
    )

    def self_attention(current):
        current = current.astype(BF).reshape(STEPS, slot_count, 3, HEADS, HD).transpose(1, 0, 2, 3, 4)
        all_keys = jnp.concatenate([cache_keys, current[:, :, 1]], axis=1)
        all_values = jnp.concatenate([cache_values, current[:, :, 2]], axis=1)
        attended = jax.vmap(attend_shared)(current[:, :, 0], all_keys, all_values, key_mask)
        return attended.transpose(1, 0, 2, 3).reshape(STEPS * slot_count, KV)

    old_keys = old_memory[:, :, :KV].reshape(OLD_DEV, SRC_MAX, HEADS, HD)
    old_values = old_memory[:, :, KV:].reshape(OLD_DEV, SRC_MAX, HEADS, HD)
    old_mask = (jnp.arange(SRC_MAX, dtype=jnp.int32)[None, :] < old_lengths[:, None]).astype(F32)

    inputs_wide = decode_inputs.astype(F32).reshape(STEPS * slot_count, -1)
    normed_inputs = normalized(decode_inputs).astype(BF).reshape(STEPS * slot_count, -1)

    def query_rows(x):
        return spread_features(normalized(inputs_wide + x).astype(BF))

    decode_stages = [
        lambda x: spread_features(x),
        lambda x: sum_in_plane(matmul(reorder(order_plain, x), qkv_weight), devices, own_index),
        lambda x: sum_planes(x, devices, own_index),
        lambda x: spread_features(self_attention(x)),
        lambda x: sum_in_plane(matmul(reorder(order_plain, x), self_out_weight), devices, own_index),
        lambda x: sum_lines(x, devices),
        lambda x: query_rows(x),
        lambda x: sum_in_plane(matmul(reorder(order_request, x), cross_query_weight), devices, own_index),
        lambda x: sum_planes(x, devices, own_index),
    ]

    sequence = [0, 1, planes // 2] + [d for d in turn_order(planes) if d not in (1, planes // 2)]
    last = len(sequence)
    state = {("pick", i): picked(sequence[i]) for i in range(2)}
    state[("at", 0)] = state.pop(("pick", 0))
    state["decode"] = decode_stages[0](normed_inputs)
    stages_of = {0: (1, 2), 1: (3,), 2: (4,), 3: (5,), 4: (6,), 7: (7, 8)}
    for phase in range(last + 5):
        keys = sorted(state, key=str)
        state = dict(zip(keys, lax.optimization_barrier(tuple(state[k] for k in keys))))
        made = {}
        for i, distance in enumerate(sequence):
            station = phase - i
            if station == -2 and i > 1 or phase == 0 and i > 2:
                made[("pick", i)] = picked(distance)
            if station == -1:
                made[("at", i)] = turn(state.pop(("pick", i)), devices, distance)
            elif station == 0:
                made[("side", i)] = swap(state[("at", i)], devices, 2)
            elif station == 1:
                made[("core", i)] = swap(state[("at", i)], devices, 1)
                made[("diagonal", i)] = swap(state[("side", i)], devices, 1)
            elif station == 2:
                partial = product(
                    jnp.concatenate([state.pop((k, i)) for k in ("at", "side", "core", "diagonal")], axis=0)
                )
                made[("own", i)] = partial
                made[("sent", i)] = partial[2 * capacity :].astype(BF)
            elif station == 3:
                made[("sent", i)] = swap(state.pop(("sent", i)), devices, 1)
            elif station == 4:
                far = state[("own", i)][capacity : 2 * capacity] + state[("sent", i)][capacity:].astype(F32)
                made[("far", i)] = swap(far.astype(BF), devices, 2)
            elif station == 5:
                full = state.pop(("own", i))[:capacity] + state.pop(("sent", i))[:capacity].astype(F32)
                full = (full + state.pop(("far", i)).astype(F32)).astype(BF)
                made[("back", i)] = turn(full, devices, planes - distance) if distance else full
        for stage in stages_of.get(phase, ()):
            state["decode"] = decode_stages[stage](state["decode"])
            if stage == 5:
                made["self_sum"] = state["decode"]
        state.update(made)
    after_self = inputs_wide + state["self_sum"]
    cross_rows = state["decode"].astype(BF).reshape(STEPS, HELD, HEADS, HD)
    back = {d: state[("back", i)] for i, d in enumerate(sequence)}
    old_out = jax.vmap(attend_shared)(
        cross_rows[:, SRC_DEV:].transpose(1, 0, 2, 3),
        old_keys,
        old_values,
        jnp.broadcast_to(old_mask[:, None, :], (OLD_DEV, STEPS, SRC_MAX)),
    ).transpose(1, 0, 2, 3)

    encoder_sum = source_tokens.astype(F32)
    for distance in distances:
        place, gate = choices[distance]
        pick = (place[:, None] == spots[None, :]).astype(BF)
        encoder_sum = encoder_sum + gate[:, None] * jnp.dot(pick, back[distance], preferred_element_type=F32)
    encoded = encoder_sum.astype(BF)
    memory = normalized(encoder_sum).astype(BF)
    memory_kv = jnp.dot(memory, memory_weight, preferred_element_type=F32).astype(BF)
    new_keys = memory_kv[:, :KV].reshape(TOK_DEV, HEADS, HD)
    new_values = memory_kv[:, KV:].reshape(TOK_DEV, HEADS, HD)
    bounds = jnp.cumsum(source_lengths[0])
    segment = jnp.sum(
        (jnp.arange(TOK_DEV, dtype=jnp.int32)[:, None] >= bounds[None, :]).astype(jnp.int32),
        axis=-1,
    )
    new_mask = (segment[None, :] == jnp.arange(SRC_DEV, dtype=jnp.int32)[:, None]).astype(F32)
    new_out = attend_shared(
        cross_rows[:, :SRC_DEV].reshape(STEPS * SRC_DEV, HEADS, HD),
        new_keys,
        new_values,
        jnp.tile(new_mask, (STEPS, 1)),
    ).reshape(STEPS, SRC_DEV, HEADS, HD)
    held_out = jnp.concatenate([new_out, old_out], axis=1).reshape(STEPS * HELD, KV)
    cross_rows_out = reorder(order_slot, spread_features(held_out))
    cross_sum = sum_planes(
        sum_in_plane(matmul(cross_rows_out, cross_out_weight), devices, own_index), devices, own_index
    )
    decoded = (after_self + cross_sum).astype(BF).reshape(STEPS, slot_count, -1)
    return (encoded, decoded)


def solution(mesh):
    return jax.shard_map(
        body,
        mesh=mesh,
        in_specs=(
            P(("group", "expert"), None),
            P(("group", "expert"), None),
            P(("group", "expert"), None),
            P(),
            P("expert", None, None),
            P("expert", None, None),
            P(),
            P(None, ("group", "expert"), None),
            P(("group", "expert"), None, None),
            P(("group", "expert")),
            P(("group", "expert"), None, None),
            P(("group", "expert")),
            P("group"),
            P("expert", None),
            P("expert", None),
            P("expert", None),
            P("expert", None),
        ),
        out_specs=(P(("group", "expert"), None), P(None, ("group", "expert"), None)),
        check_vma=False,
    )
```

```python
import jax
import jax.numpy as jnp
from jax import lax
from jax.sharding import PartitionSpec as P

HEADS = 8
HD = 128
EXP_SPLIT = 4
SRC_DEV = 4
OLD_DEV = 2
TOK_DEV = 256
CTX = 64
KV = 1024
SRC_MAX = 192
HELD = 6
STEPS = 2
BF = jnp.bfloat16
F32 = jnp.float32


def normalized(values):
    values = values.astype(jnp.float32)
    average = jnp.mean(values, axis=-1, keepdims=True)
    centred = values - average
    variance = jnp.mean(centred * centred, axis=-1, keepdims=True)
    return centred * lax.rsqrt(variance + 1e-05)


def attend_shared(queries, all_keys, all_values, key_mask):
    scores = jnp.einsum("phd,jhd->phj", queries, all_keys, preferred_element_type=F32) * HD ** (-0.5)
    raised = jnp.exp(scores) * key_mask[:, None, :]
    weights_bf = (raised / jnp.sum(raised, axis=-1, keepdims=True)).astype(BF)
    result = jnp.einsum("phj,jhd->phd", weights_bf, all_values, preferred_element_type=F32)
    return result.astype(BF)


def swap(values, devices, bit):
    return lax.ppermute(values, "expert", [(i, i ^ bit) for i in range(devices)])


def turn(values, devices, distance):
    step = EXP_SPLIT * distance
    return lax.ppermute(values, "expert", [(i, (i + step) % devices) for i in range(devices)])


def turn_order(planes):
    order = []
    for distance in range(1, planes // 2 + 1):
        order.append(distance)
        if planes - distance != distance:
            order.append(planes - distance)
    return order


def rows_at(values, index, count):
    return lax.dynamic_slice_in_dim(values, index * count, count, 0)


def sum_in_plane(partial, devices, own_index):
    core = own_index % 2
    side = (own_index // 2) % 2
    count = partial.shape[0] // 2
    sent = rows_at(partial, 1 - core, count).astype(BF)
    kept = rows_at(partial, core, count) + swap(sent, devices, 1).astype(F32)
    count = count // 2
    sent = rows_at(kept, 1 - side, count).astype(BF)
    return rows_at(kept, side, count) + swap(sent, devices, 2).astype(F32)


def sum_planes(kept, devices, own_index):
    planes = devices // EXP_SPLIT
    plane = own_index // EXP_SPLIT
    count = kept.shape[0] // planes
    total = rows_at(kept, plane, count)
    low = kept.astype(BF)
    for distance in turn_order(planes):
        total = total + turn(rows_at(low, (plane + distance) % planes, count), devices, distance).astype(F32)
    return total


def sum_lines(kept, devices):
    planes = devices // EXP_SPLIT
    lines = [[plane * EXP_SPLIT + place for plane in range(planes)] for place in range(EXP_SPLIT)]
    parts = lax.all_to_all(
        kept.astype(BF), "expert", split_axis=0, concat_axis=0, tiled=True, axis_index_groups=lines
    )
    return jnp.sum(parts.reshape(planes, -1, kept.shape[1]).astype(F32), axis=0)


def spread_features(local_rows):
    return lax.all_to_all(local_rows, "expert", split_axis=1, concat_axis=0, tiled=True)


def reorder(order, spread):
    return jnp.dot(order, spread, preferred_element_type=F32).astype(BF)


def matmul(left, right):
    return jnp.dot(left, right, preferred_element_type=F32)


def body(
    source_tokens,
    routes,
    source_lengths,
    router_weight,
    expert_in,
    expert_out,
    memory_weight,
    decode_inputs,
    self_cache,
    context_lengths,
    old_memory,
    old_lengths,
    slot_of,
    qkv_weight,
    self_out_weight,
    cross_query_weight,
    cross_out_weight,
):
    devices = lax.axis_size("expert")
    own_index = lax.axis_index("expert")
    token_count = source_tokens.shape[0]
    expert_count = router_weight.shape[1]
    planes = devices // EXP_SPLIT
    plane = own_index // EXP_SPLIT
    capacity = 3 * token_count // expert_count
    slot_count = decode_inputs.shape[1]

    hidden_rows = normalized(source_tokens).astype(BF)
    logits = jnp.dot(hidden_rows, router_weight, preferred_element_type=F32)
    one_hot = routes[:, :, None] == jnp.arange(expert_count, dtype=jnp.int32)[None, None, :]
    chosen = jnp.sum(jnp.where(one_hot, logits[:, None, :], 0.0), axis=-1)
    leading = jax.nn.sigmoid(chosen[:, 0] - chosen[:, 1])
    member = jnp.any(one_hot, axis=1)
    earlier = (
        jnp.arange(token_count, dtype=jnp.int32)[:, None] > jnp.arange(token_count, dtype=jnp.int32)[None, :]
    ).astype(BF)
    rank = jnp.dot(earlier, member.astype(BF), preferred_element_type=F32).astype(jnp.int32)
    w_in = expert_in[0]
    w_out = expert_out[0]

    def choice(distance):
        target = (plane + distance) % planes
        is_target = jnp.arange(expert_count, dtype=jnp.int32) == target
        there = jnp.any(member & is_target[None, :], axis=1)
        place = jnp.sum(jnp.where(is_target[None, :], rank, 0), axis=1)
        place = jnp.where(there, place, -1)
        gate = jnp.where(routes[:, 0] == target, leading, 0.0) + jnp.where(
            routes[:, 1] == target, 1.0 - leading, 0.0
        )
        return place, gate

    distances = turn_order(planes) + [0]
    spots = jnp.arange(capacity, dtype=jnp.int32)
    choices = {d: choice(d) for d in distances}

    def picked(distance):
        place, _ = choices[distance]
        pick = (place[None, :] == spots[:, None]).astype(BF)
        return jnp.dot(pick, hidden_rows, preferred_element_type=F32).astype(BF)

    def product(rows):
        return matmul(jnp.maximum(matmul(rows, w_in), 0.0).astype(BF), w_out)

    global_slots = own_index * slot_count + jnp.arange(slot_count, dtype=jnp.int32)
    new_slots = slot_of.reshape(devices, HELD)[:, :SRC_DEV].reshape(-1)
    fresh_slot = jnp.any(global_slots[:, None] == new_slots[None, :], axis=-1)
    effective = jnp.where(fresh_slot, 0, context_lengths)
    cache_mask = (jnp.arange(CTX, dtype=jnp.int32)[None, :] < effective[:, None]).astype(F32)
    cache_keys = self_cache[:, :, :KV].reshape(slot_count, CTX, HEADS, HD)
    cache_values = self_cache[:, :, KV:].reshape(slot_count, CTX, HEADS, HD)
    count = slot_of.shape[0]
    to_request = (slot_of[:, None] == jnp.arange(count, dtype=jnp.int32)[None, :]).astype(BF)

    row = jnp.arange(STEPS * count, dtype=jnp.int32)
    held = STEPS * HELD
    target = row // held
    target_device = target % planes * EXP_SPLIT + target // planes % 2 * 2 + target // (2 * planes)
    target_row = target_device * held + row % held

    def source_of(rows):
        slots = slot_of[rows // held * HELD + rows % HELD]
        return slots // HELD * held + rows // HELD % STEPS * HELD + slots % HELD

    order_plain = (target_row[:, None] == row[None, :]).astype(BF)
    order_request = (source_of(target_row)[:, None] == row[None, :]).astype(BF)
    order_slot = (target_row[:, None] == source_of(row)[None, :]).astype(BF)
    steps = jnp.arange(STEPS, dtype=jnp.int32)
    causal = (steps[:, None] >= steps[None, :]).astype(F32)
    key_mask = jnp.concatenate(
        [
            jnp.broadcast_to(cache_mask[:, None, :], (slot_count, STEPS, CTX)),
            jnp.broadcast_to(causal[None], (slot_count, STEPS, STEPS)),
        ],
        axis=2,
    )

    def self_attention(current):
        current = current.astype(BF).reshape(STEPS, slot_count, 3, HEADS, HD).transpose(1, 0, 2, 3, 4)
        all_keys = jnp.concatenate([cache_keys, current[:, :, 1]], axis=1)
        all_values = jnp.concatenate([cache_values, current[:, :, 2]], axis=1)
        attended = jax.vmap(attend_shared)(current[:, :, 0], all_keys, all_values, key_mask)
        return attended.transpose(1, 0, 2, 3).reshape(STEPS * slot_count, KV)

    old_keys = old_memory[:, :, :KV].reshape(OLD_DEV, SRC_MAX, HEADS, HD)
    old_values = old_memory[:, :, KV:].reshape(OLD_DEV, SRC_MAX, HEADS, HD)
    old_mask = (jnp.arange(SRC_MAX, dtype=jnp.int32)[None, :] < old_lengths[:, None]).astype(F32)

    inputs_wide = decode_inputs.astype(F32).reshape(STEPS * slot_count, -1)
    normed_inputs = normalized(decode_inputs).astype(BF).reshape(STEPS * slot_count, -1)

    def query_rows(x):
        return spread_features(normalized(inputs_wide + x).astype(BF))

    decode_stages = [
        lambda x: spread_features(x),
        lambda x: sum_in_plane(matmul(reorder(order_plain, x), qkv_weight), devices, own_index),
        lambda x: sum_planes(x, devices, own_index),
        lambda x: spread_features(self_attention(x)),
        lambda x: sum_in_plane(matmul(reorder(order_plain, x), self_out_weight), devices, own_index),
        lambda x: sum_lines(x, devices),
        lambda x: query_rows(x),
        lambda x: sum_in_plane(matmul(reorder(order_request, x), cross_query_weight), devices, own_index),
        lambda x: sum_planes(x, devices, own_index),
    ]

    sequence = [0, 1, planes // 2] + [d for d in turn_order(planes) if d not in (1, planes // 2)]
    last = len(sequence)
    state = {("pick", i): picked(sequence[i]) for i in range(2)}
    state[("at", 0)] = state.pop(("pick", 0))
    state["decode"] = decode_stages[0](normed_inputs)
    stages_of = {0: (1, 2), 1: (3,), 2: (4,), 3: (5,), 4: (6,), 7: (7, 8)}
    for phase in range(last + 5):
        keys = sorted(state, key=str)
        state = dict(zip(keys, lax.optimization_barrier(tuple(state[k] for k in keys))))
        made = {}
        for i, distance in enumerate(sequence):
            station = phase - i
            if station == -2 and i > 1 or phase == 0 and i > 2:
                made[("pick", i)] = picked(distance)
            if station == -1:
                made[("at", i)] = turn(state.pop(("pick", i)), devices, distance)
            elif station == 0:
                made[("side", i)] = swap(state[("at", i)], devices, 2)
                made[("core", i)] = swap(state[("at", i)], devices, 1)
            elif station == 1:
                made[("diagonal", i)] = swap(state[("side", i)], devices, 1)
            elif station == 2:
                partial = product(
                    jnp.concatenate([state.pop((k, i)) for k in ("at", "side", "core", "diagonal")], axis=0)
                )
                made[("own", i)] = partial
                made[("sent", i)] = partial[2 * capacity :].astype(BF)
            elif station == 3:
                made[("sent", i)] = swap(state.pop(("sent", i)), devices, 1)
            elif station == 4:
                far = state[("own", i)][capacity : 2 * capacity] + state[("sent", i)][capacity:].astype(F32)
                made[("far", i)] = swap(far.astype(BF), devices, 2)
            elif station == 5:
                full = state.pop(("own", i))[:capacity] + state.pop(("sent", i))[:capacity].astype(F32)
                full = (full + state.pop(("far", i)).astype(F32)).astype(BF)
                made[("back", i)] = turn(full, devices, planes - distance) if distance else full
        for stage in stages_of.get(phase, ()):
            state["decode"] = decode_stages[stage](state["decode"])
            if stage == 5:
                made["self_sum"] = state["decode"]
        state.update(made)
    after_self = inputs_wide + state["self_sum"]
    cross_rows = state["decode"].astype(BF).reshape(STEPS, HELD, HEADS, HD)
    back = {d: state[("back", i)] for i, d in enumerate(sequence)}
    old_out = jax.vmap(attend_shared)(
        cross_rows[:, SRC_DEV:].transpose(1, 0, 2, 3),
        old_keys,
        old_values,
        jnp.broadcast_to(old_mask[:, None, :], (OLD_DEV, STEPS, SRC_MAX)),
    ).transpose(1, 0, 2, 3)

    encoder_sum = source_tokens.astype(F32)
    for distance in distances:
        place, gate = choices[distance]
        pick = (place[:, None] == spots[None, :]).astype(BF)
        encoder_sum = encoder_sum + gate[:, None] * jnp.dot(pick, back[distance], preferred_element_type=F32)
    encoded = encoder_sum.astype(BF)
    memory = normalized(encoder_sum).astype(BF)
    memory_kv = jnp.dot(memory, memory_weight, preferred_element_type=F32).astype(BF)
    new_keys = memory_kv[:, :KV].reshape(TOK_DEV, HEADS, HD)
    new_values = memory_kv[:, KV:].reshape(TOK_DEV, HEADS, HD)
    bounds = jnp.cumsum(source_lengths[0])
    segment = jnp.sum(
        (jnp.arange(TOK_DEV, dtype=jnp.int32)[:, None] >= bounds[None, :]).astype(jnp.int32),
        axis=-1,
    )
    new_mask = (segment[None, :] == jnp.arange(SRC_DEV, dtype=jnp.int32)[:, None]).astype(F32)
    new_out = attend_shared(
        cross_rows[:, :SRC_DEV].reshape(STEPS * SRC_DEV, HEADS, HD),
        new_keys,
        new_values,
        jnp.tile(new_mask, (STEPS, 1)),
    ).reshape(STEPS, SRC_DEV, HEADS, HD)
    held_out = jnp.concatenate([new_out, old_out], axis=1).reshape(STEPS * HELD, KV)
    cross_rows_out = reorder(order_slot, spread_features(held_out))
    cross_sum = sum_planes(
        sum_in_plane(matmul(cross_rows_out, cross_out_weight), devices, own_index), devices, own_index
    )
    decoded = (after_self + cross_sum).astype(BF).reshape(STEPS, slot_count, -1)
    return (encoded, decoded)


def solution(mesh):
    return jax.shard_map(
        body,
        mesh=mesh,
        in_specs=(
            P(("group", "expert"), None),
            P(("group", "expert"), None),
            P(("group", "expert"), None),
            P(),
            P("expert", None, None),
            P("expert", None, None),
            P(),
            P(None, ("group", "expert"), None),
            P(("group", "expert"), None, None),
            P(("group", "expert")),
            P(("group", "expert"), None, None),
            P(("group", "expert")),
            P("group"),
            P("expert", None),
            P("expert", None),
            P("expert", None),
            P("expert", None),
        ),
        out_specs=(P(("group", "expert"), None), P(None, ("group", "expert"), None)),
        check_vma=False,
    )
```
